256 devices in a mesh: row: 16 (over x, z_hi), col: 16 (over y, z_lo, core).
Axes of the slice: x: 4, y: 4, z: 8 (z_hi: 4, z_lo: 2; z = z_hi * 2 + z_lo), core: 2. Of those that a mesh axis runs over, the one named last changes fastest.
Arguments:
- pair: bfloat16 [640, 640, 128], P('row', 'col'), may hold values from -6 to 6
- token_mask: int32 [640], replicated, may hold values from 0 to 1, as said below
- chain_ids: int32 [640], replicated, may hold values from 0 to 7, never falling along the last dimension, each value on 1 to 160 neighbouring positions
- chain_bias: float32 [128], replicated, may hold values from -4 to 4
- in_weights: bfloat16 [2, 128, 640], replicated, may hold values from -0.5 to 0.5
- out_weights: bfloat16 [2, 128, 128], replicated, may hold values from -0.5 to 0.5
Outputs:
- pair_out: bfloat16 [640, 640, 128], P('row', 'col')
The draws below stay inside these ranges and needn't reach their ends.
Inputs may be any that keep to these rules, and one draw needn't show every extreme that they name: token_mask is 0 on a run of padding at the end that always includes the last token; some tokens before it may be 0 as well. chain_ids never falls along the tokens.
All inputs are finite; a program needn't handle non-finite values.
Results may differ from the reference program's by a relative error of at most 0.015.
Values may be sent and summed in bfloat16 or wider, within the bound.
A program may use at most 128 MiB of HBM per device.

```python
import math
import jax
import jax.numpy as jnp
import numpy as np
from jax import lax

CHANNELS = 128
TOK_ROW = 40
CHAINS = 8
TOKENS = 640
TILE_COL = 40


def draw_token_mask(key, part):
    key = jax.random.fold_in(key, 3)
    length_key, hole_key = jax.random.split(key)
    length = jax.random.randint(length_key, (), TOKENS - TOKENS // 8, TOKENS)
    holes = jax.random.randint(hole_key, (TOKENS,), 0, 16)
    kept = (jnp.arange(TOKENS) < length) & (holes != 0)
    return kept.astype(jnp.int32)


def block_levels(rng, dims, cuts, smallest, high):
    loudness, own = 1.0, jax.random.fold_in(rng, 6)
    for dim, blocks in cuts:
        draws = jnp.exp(jax.random.uniform(jax.random.fold_in(own, dim), (blocks,), jnp.float32, smallest / len(cuts), high / len(cuts)))
        loudness = loudness * jnp.repeat(draws, dims[dim] // blocks).reshape([-1 if axis == dim else 1 for axis in range(len(dims))])
    return loudness


def profile(number_of, total, reach, slope):
    weights = [(1 << 20) // math.isqrt(grade ** slope) + 1 for grade in range(2, number_of + 1)]
    spare, holding = total - reach - (number_of - 1), [1] * (number_of - 1)
    while spare > 0:
        free = [i for i in range(number_of - 1) if holding[i] < reach]
        mass, left = sum([weights[i] for i in free]), spare
        for i in free:
            more = min(reach - holding[i], max(1, left * weights[i] // mass), spare)
            holding[i] = holding[i] + more
            spare = spare - more
    return np.array([reach] + holding)


def ragged_sizes(stream_key, amount, total, limit, skew):
    if amount == 2:
        one = jax.random.randint(stream_key, (), max(1, total - limit), min(limit, total - 1) + 1)
        return jnp.stack([one, total - one])
    sizes = jnp.asarray(profile(amount, total, limit, skew), jnp.int32)
    pairs = (amount - 1) // 2
    giver, taker = sizes[1:1 + 2 * pairs:2], sizes[2:2 + 2 * pairs:2]
    margin = jnp.minimum(giver - 1, limit - taker)
    moved = jax.random.randint(jax.random.fold_in(stream_key, 1), (pairs,), 0, 1 << 20) % (margin + 1)
    sizes = sizes.at[1:1 + 2 * pairs:2].set(giver - moved).at[2:2 + 2 * pairs:2].set(taker + moved)
    return sizes[jax.random.permutation(jax.random.fold_in(stream_key, 2), amount)]


def gaussian(rng, shape, deviation, reach, cuts=(), kind=jnp.bfloat16):
    result = jax.random.normal(rng, shape, jnp.float32) * deviation
    if len(cuts) > 0:
        result = block_levels(rng, shape, cuts, -0.22, 0.18) * result
    return jnp.clip(result, min=-reach, max=reach).astype(kind)


def setup_inputs(seed: int = 0) -> dict:
    key_of = jax.random.split(jax.random.key(seed), 7)
    return {
        "pair": gaussian(key_of[0], (TOKENS, TOKENS, CHANNELS), 1.0, 6.0, ((0, 16), (1, 16))),
        "token_mask": draw_token_mask(jax.random.fold_in(key_of[6], 71), 0),
        "chain_ids": jnp.searchsorted(jnp.cumsum(ragged_sizes(key_of[2], CHAINS, TOKENS, TOKENS // 4, 1)), jnp.arange(TOKENS), side="right").astype(jnp.int32),
        "chain_bias": gaussian(key_of[3], (CHANNELS,), 1.0, 4.0, (), jnp.float32),
        "in_weights": gaussian(key_of[4], (2, CHANNELS, 5 * CHANNELS), CHANNELS ** -0.5, 0.5),
        "out_weights": gaussian(key_of[5], (2, CHANNELS, CHANNELS), CHANNELS ** -0.5, 0.5),
    }


def layer_norm(values):
    center = values - lax.optimization_barrier(jnp.mean(values, axis=-1, keepdims=True))
    spread = lax.optimization_barrier(jnp.mean(center * center, axis=-1, keepdims=True))
    return center * lax.rsqrt(spread + 1e-05)

def rounded(values):
    return lax.optimization_barrier(values.astype(jnp.bfloat16)).astype(jnp.float32)

def reference(pair, token_mask, chain_ids, chain_bias, in_weights, out_weights):
    valid = token_mask.astype(jnp.float32)
    pair_mask = valid[:, None] * valid[None, :]
    same_chain = (chain_ids[:, None] == chain_ids[None, :]).astype(jnp.float32)
    field = pair.astype(jnp.float32) + same_chain[:, :, None] * chain_bias
    for direction in range(2):
        normed = layer_norm(field).astype(jnp.bfloat16)
        projected = jnp.dot(normed.reshape(-1, CHANNELS), in_weights[direction], preferred_element_type=jnp.float32)
        projected = projected.reshape(TOKENS, TOKENS, 5 * CHANNELS)
        width = CHANNELS
        first = (jax.nn.sigmoid(projected[..., :width]) * projected[..., width:2 * width] * pair_mask[:, :, None]).astype(jnp.bfloat16)
        second = (jax.nn.sigmoid(projected[..., 2 * width:3 * width]) * projected[..., 3 * width:4 * width] * pair_mask[:, :, None]).astype(jnp.bfloat16)
        gate_value = jax.nn.sigmoid(projected[..., 4 * width:])
        first_wide = first.astype(jnp.float32)
        second_wide = second.astype(jnp.float32)
        summed = jnp.zeros((TOKENS, TOKENS, CHANNELS), jnp.float32)
        if direction == 0:
            block = TILE_COL
            for index in range(TOKENS // block):
                lo = index * block
                part = jnp.einsum('ikc,jkc->ijc', first_wide[:, lo:lo + block], second_wide[:, lo:lo + block], precision=lax.Precision.HIGHEST)
                summed = summed + rounded(part)
        else:
            block = TOK_ROW
            for index in range(TOKENS // block):
                lo = index * block
                part = jnp.einsum('kic,kjc->ijc', first_wide[lo:lo + block], second_wide[lo:lo + block], precision=lax.Precision.HIGHEST)
                summed = summed + rounded(part)
        normed_sum = layer_norm(summed).astype(jnp.bfloat16)
        output = jnp.dot(normed_sum.reshape(-1, CHANNELS), out_weights[direction], preferred_element_type=jnp.float32)
        field = field + gate_value * output.reshape(TOKENS, TOKENS, CHANNELS)
    return field.astype(jnp.bfloat16)
```

```python
import functools

import jax
import jax.numpy as jnp
from jax import lax
from jax.experimental import pallas as pl
from jax.experimental.pallas import tpu as pltpu
from jax.sharding import PartitionSpec as P


MESH = pl.DeviceIdType.MESH
TOK = 40
ROWS = 16
PLANE = 8
CHIPS = ROWS * PLANE
CH = 128
PERM = 16 * 128
BF = jnp.bfloat16
F32 = jnp.float32
VMEM_LIMIT = 40 * 2**20


def sigmoid(x):
    return 0.5 * jnp.tanh(0.5 * x) + 0.5


def norm_lanes(x):
    center = x - jnp.mean(x, axis=-1, keepdims=True)
    spread = jnp.mean(center * center, axis=-1, keepdims=True)
    return center * lax.rsqrt(spread + 1e-05)


def start_field(pair_ref, chain_rows_ref, chain_cols_ref, bias_ref, field_ref):
    bias = bias_ref[...]
    cols = chain_cols_ref[...]
    for i in range(TOK):
        same = cols == chain_rows_ref[i]
        field_ref[pl.ds(i * TOK, TOK)] = pair_ref[i].astype(F32) + jnp.where(same, bias, 0.0)


def produce(field_ref, w_ref, mask_ref, f_ref, s_ref, gate_ref, nat, perm, tiles, swap):
    nat[...] = norm_lanes(field_ref[...])
    for g in range(16):
        for q in range(3):
            a = 16 * q + g
            at = pl.ds(g * 128 + TOK * q, TOK)
            if a >= TOK:
                perm[at] = jnp.zeros((TOK, CH), F32)
            elif swap:
                perm[at] = nat[pl.ds(a, TOK, stride=TOK)]
            else:
                perm[at] = nat[pl.ds(a * TOK, TOK)]
        perm[pl.ds(g * 128 + 120, 8)] = jnp.zeros((8, CH), F32)
    weights_t = jnp.transpose(w_ref[...].astype(F32)).astype(BF)
    for half, out in enumerate((f_ref, s_ref)):
        for part in range(4):
            lo = part * 512
            normed = perm[pl.ds(lo, 512)].astype(BF)
            both = lax.dot_general(
                weights_t[half * 256 : half * 256 + 256], normed, (((1,), (1,)), ((), ())), preferred_element_type=F32
            )
            value = sigmoid(both[:CH]) * both[CH:]
            for n in range(4):
                g = part * 4 + n
                tiles[pl.ds(g, CH, stride=16)] = value[:, n * 128 : n * 128 + 128] * mask_ref[g : g + 1, :]
        out[...] = tiles[...].reshape(CH, 16, 128).astype(BF)
    for part in range(4):
        normed = perm[pl.ds(part * 512, 512)].astype(BF)
        value = sigmoid(jnp.dot(normed, w_ref[:, 512:640], preferred_element_type=F32))
        for n in range(4):
            for q in range(3):
                a = 16 * q + part * 4 + n
                if a < TOK:
                    piece = value[n * 128 + q * TOK : n * 128 + q * TOK + TOK]
                    if swap:
                        gate_ref[pl.ds(a, TOK, stride=TOK)] = piece
                    else:
                        gate_ref[pl.ds(a * TOK, TOK)] = piece


def finish(field_ref, gate_ref, r_ref, w_ref, tiles):
    x = r_ref[...].astype(F32)
    center = x - jnp.mean(x, axis=0, keepdims=True)
    spread = jnp.mean(center * center, axis=0, keepdims=True)
    tiles[...] = (center * lax.rsqrt(spread + 1e-05)).reshape(CH * 16, 128)
    weights = w_ref[...]
    for g in range(16):
        normed = tiles[pl.ds(g, CH, stride=16)].astype(BF)
        out = lax.dot_general(normed, weights, (((0,), (0,)), ((), ())), preferred_element_type=F32)
        for q in range(3):
            a = 16 * q + g
            if a < TOK:
                at = pl.ds(a * TOK, TOK)
                field_ref[at] = field_ref[at] + gate_ref[at] * out[q * TOK : q * TOK + TOK]


def lanes_between(lo, hi, rows):
    lane = lax.broadcasted_iota(jnp.int32, (rows, 128), 1)
    return (lane >= lo) & (lane < hi)


def roll(x, amount):
    amount = amount % 128
    return pltpu.roll(x, amount, 1) if amount else x


def spread_lanes(blocks, q, rows):
    total = jnp.zeros((rows, 128), F32)
    for m, block in enumerate(blocks):
        total = jnp.where(lanes_between(TOK * m, TOK * m + TOK, rows), roll(block, TOK * (m - q)), total)
    return total


def triangle(load_m, load_n, out_ref, left, right, part):
    part[...] = jnp.zeros((384, 128), F32)
    for group in range(6):
        blocks = range(3 * group, min(3 * group + 3, 16))
        lane = pl.ds(group * 128, 128)
        m_blocks = [load_m(k).astype(F32) for k in blocks]
        n_blocks = [load_n(k).astype(F32) for k in blocks]
        for q in range(3):
            left[pl.ds(q * 256, 256), lane] = spread_lanes(m_blocks, q, 256).astype(BF)
            value = spread_lanes(n_blocks, q, 128)
            for n in range(8):
                depth = 16 if q < 2 else 8
                part[pl.ds(128 * (n // 3) + TOK * (n % 3) + 16 * q, depth)] = value[n * 16 : n * 16 + depth]
        right[:, lane] = part[...].astype(BF)
    for n3 in range(3):
        total = lax.dot_general(
            left[...], right[pl.ds(n3 * 128, 128)], (((1,), (1,)), ((), ())), preferred_element_type=F32
        )
        for m in range(3 if n3 < 2 else 2):
            value = jnp.zeros((256, 128), F32)
            for q in range(3):
                value = jnp.where(
                    lanes_between(TOK * q, TOK * q + TOK, 256),
                    roll(total[q * 256 : q * 256 + 256], TOK * (q - m)),
                    value,
                )
            out_ref[3 * n3 + m] = value.reshape(16, 16, 128).astype(BF)


def place():
    row, col = lax.axis_index("row"), lax.axis_index("col")
    return row, col // 2, col % 2


def enter(sibling):
    row, chip, core = place()
    barrier = pltpu.get_barrier_semaphore()

    def signal(step, carry):
        to_row = (row + step // PLANE) % ROWS
        to_chip = (chip + step % PLANE) % PLANE
        pl.semaphore_signal(barrier, inc=1, device_id=(to_row, to_chip * 2 + core), device_id_type=MESH)
        return carry

    lax.fori_loop(1, CHIPS, signal, 0)
    if sibling:
        pl.semaphore_signal(barrier, inc=1, device_id=(row, chip * 2 + 1 - core), device_id_type=MESH)
    pl.semaphore_wait(barrier, CHIPS if sibling else CHIPS - 1)


def send_all(src, dst, send_sem, recv_sem):
    row, chip, core = place()
    pltpu.make_async_copy(src(row, chip), dst, recv_sem).start()

    def send(step, carry):
        to_row = (row + step // PLANE) % ROWS
        to_chip = (chip + step % PLANE) % PLANE
        pltpu.make_async_remote_copy(
            src_ref=src(to_row, to_chip),
            dst_ref=dst,
            send_sem=send_sem,
            recv_sem=recv_sem,
            device_id=(to_row, to_chip * 2 + core),
            device_id_type=MESH,
        ).start()
        return carry

    lax.fori_loop(1, CHIPS, send, 0)


def wait_bytes(ref, sem):
    pltpu.make_async_copy(ref, ref, sem).wait()


def to_sibling(ref, send_sem, recv_sem):
    row, chip, core = place()
    copy = pltpu.make_async_remote_copy(
        src_ref=ref,
        dst_ref=ref,
        send_sem=send_sem,
        recv_sem=recv_sem,
        device_id=(row, chip * 2 + 1 - core),
        device_id_type=MESH,
    )
    copy.start()
    return copy


def scatter_out(f_ref, s_ref, rf, rs, f_send, f_recv, s_send, s_recv, on_send, on_recv):
    row, chip, core = place()
    enter(True)
    index = row * PLANE + chip
    send_all(lambda r, c: f_ref.at[r * PLANE + c], rf.at[core, chip, row], f_send, f_recv)
    send_all(
        lambda r, c: s_ref.at[r * PLANE + c], rs.at[row % 2, core, chip, row // 2], s_send, s_recv.at[row % 2]
    )
    wait_bytes(rf.at[0], f_recv)
    copy_f = to_sibling(rf.at[core], on_send.at[0], on_recv.at[0])
    wait_bytes(rs.at[0, 0], s_recv.at[1 - core])
    copy_s = to_sibling(rs.at[1 - core, core], on_send.at[1], on_recv.at[1])
    wait_bytes(rs.at[0, 0], s_recv.at[core])
    copy_f.wait()
    copy_s.wait()
    wait_bytes(f_ref.at[pl.ds(0, CHIPS - 1)], f_send)
    wait_bytes(f_ref.at[pl.ds(0, CHIPS - 1)], s_send)


def scatter_in(f_ref, s_ref, rf, rs, f_send, f_recv, s_send, s_recv, on_send, on_recv):
    row, chip, core = place()
    enter(True)
    send_all(lambda r, c: f_ref.at[r * PLANE + c], rf.at[core, row, chip], f_send, f_recv)
    send_all(lambda r, c: s_ref.at[r * PLANE + c], rs.at[row, chip], s_send, s_recv)
    wait_bytes(rf.at[0], f_recv)
    copy_f = to_sibling(rf.at[core], on_send, on_recv)
    wait_bytes(rs, s_recv)
    copy_f.wait()
    wait_bytes(f_ref.at[pl.ds(0, CHIPS - 1)], f_send)
    wait_bytes(f_ref.at[pl.ds(0, CHIPS - 1)], s_send)


def bring_back(incoming, o_ref, r_ref, send_sem, recv_sem):
    row, chip, core = place()
    enter(False)
    if incoming:
        src = lambda r, c: o_ref.at[c, (r % 2) * PLANE + r // 2]
    else:
        src = lambda r, c: o_ref.at[c, r]
    send_all(src, r_ref.at[row * PLANE + chip], send_sem, recv_sem)
    wait_bytes(r_ref, recv_sem)
    wait_bytes(r_ref.at[pl.ds(0, CHIPS - 1)], send_sem)


def first_kernel(pair_ref, rows_ref, cols_ref, bias_ref, w_ref, mask_ref, f_ref, s_ref, gate_ref, field_ref, nat, perm, tiles):
    start_field(pair_ref, rows_ref, cols_ref, bias_ref, field_ref)
    produce(field_ref, w_ref, mask_ref, f_ref, s_ref, gate_ref, nat, perm, tiles, False)


def middle_kernel(
    field_ref, gate_ref, r_ref, wo_ref, w_ref, mask_ref, f_ref, s_ref, gate2_ref, field2_ref, nat, perm, tiles
):
    field2_ref[...] = field_ref[...]
    finish(field2_ref, gate_ref, r_ref, wo_ref, tiles)
    produce(field2_ref, w_ref, mask_ref, f_ref, s_ref, gate2_ref, nat, perm, tiles, True)


def last_kernel(field_ref, gate_ref, r_ref, wo_ref, out_ref, field2, tiles):
    field2[...] = field_ref[...]
    finish(field2, gate_ref, r_ref, wo_ref, tiles)
    for i in range(TOK):
        out_ref[i] = field2[pl.ds(i * TOK, TOK)].astype(BF)


def triangle_out_kernel(rf, rs, o_ref, left, right, part):
    core = lax.axis_index("col") % 2
    triangle(
        lambda k: rf[k % 2, k // 2].reshape(256, 128),
        lambda k: rs[core, k % 2, k // 2].reshape(128, 128),
        o_ref,
        left,
        right,
        part,
    )


def triangle_in_kernel(rf, rs, o_ref, left, right, part):
    triangle(
        lambda k: jnp.concatenate([rf[0, k], rf[1, k]], axis=0).reshape(256, 128),
        lambda k: rs[k].reshape(128, 128),
        o_ref,
        left,
        right,
        part,
    )


def call(kernel, outs, args, scratch, name, collective=None, smem=()):
    outs = [jax.ShapeDtypeStruct(shape, dtype) for shape, dtype in outs]
    params = dict(vmem_limit_bytes=VMEM_LIMIT)
    if collective is not None:
        params.update(collective_id=collective, has_side_effects=True)
    return pl.pallas_call(
        kernel,
        out_shape=outs,
        in_specs=[
            pl.BlockSpec(memory_space=pltpu.SMEM if i in smem else pltpu.VMEM) for i in range(len(args))
        ],
        out_specs=[pl.BlockSpec(memory_space=pltpu.VMEM)] * len(outs),
        scratch_shapes=scratch,
        compiler_params=pltpu.CompilerParams(**params),
        name=name,
    )(*args)


def tile_mask(a_valid, b_valid):
    a = jnp.pad(a_valid, (0, 8)).reshape(3, 16).T
    return jnp.pad((a[:, :, None] * b_valid[None, None, :]).reshape(16, 120), ((0, 0), (0, 8)))


def per_device(pair, token_mask, chain_ids, chain_bias, in_weights, out_weights):
    row_start = lax.axis_index("row") * TOK
    col_start = lax.axis_index("col") * TOK
    valid_rows = lax.dynamic_slice_in_dim(token_mask, row_start, TOK).astype(F32)
    valid_cols = lax.dynamic_slice_in_dim(token_mask, col_start, TOK).astype(F32)
    chain_rows = lax.dynamic_slice_in_dim(chain_ids, row_start, TOK)
    chain_cols = lax.dynamic_slice_in_dim(chain_ids, col_start, TOK)
    mask_out = tile_mask(valid_rows, valid_cols)
    mask_in = tile_mask(valid_cols, valid_rows)
    chain_cols = jnp.broadcast_to(chain_cols[:, None], (TOK, CH))

    tile = ((CH, 16, 128), BF)
    tokens = ((TOK * TOK, CH), F32)
    work = [pltpu.VMEM((TOK * TOK, CH), F32), pltpu.VMEM((PERM, CH), F32), pltpu.VMEM((PERM, CH), F32)]
    product = [pltpu.VMEM((768, 768), BF), pltpu.VMEM((384, 768), BF), pltpu.VMEM((384, 128), F32)]
    dma = pltpu.SemaphoreType.DMA

    first, second, gate, field = call(
        first_kernel,
        [tile, tile, tokens, tokens],
        [pair, chain_rows, chain_cols, chain_bias.reshape(1, CH), in_weights[0], mask_out],
        work,
        "project_out",
        smem=(1,),
    )
    rf, rs = call(
        scatter_out,
        [((2, 8, 16, 16, 128), BF), ((2, 2, 8, 8, 16, 128), BF)],
        [first, second],
        [dma, dma, dma, dma((2,)), dma((2,)), dma((2,))],
        "scatter_out",
        0,
    )
    (made,) = call(triangle_out_kernel, [((8, 16, 16, 128), BF)], [rf, rs], product, "triangle_out")
    (back,) = call(functools.partial(bring_back, False), [tile], [made], [dma, dma], "back_out", 1)
    first, second, gate, field = call(
        middle_kernel,
        [tile, tile, tokens, tokens],
        [field, gate, back, out_weights[0], in_weights[1], mask_in],
        work,
        "project_in",
    )
    rf, rs = call(
        scatter_in,
        [((2, 16, 8, 16, 128), BF), ((16, 8, 16, 128), BF)],
        [first, second],
        [dma, dma, dma, dma, dma, dma],
        "scatter_in",
        2,
    )
    (made,) = call(triangle_in_kernel, [((8, 16, 16, 128), BF)], [rf, rs], product, "triangle_in")
    (back,) = call(functools.partial(bring_back, True), [tile], [made], [dma, dma], "back_in", 3)
    (out,) = call(
        last_kernel,
        [((TOK, TOK, CH), BF)],
        [field, gate, back, out_weights[1]],
        [work[0], work[1]],
        "finish",
    )
    return out


def solution(mesh):
    return jax.shard_map(
        per_device,
        mesh=mesh,
        in_specs=(P("row", "col", None), P(), P(), P(), P(), P()),
        out_specs=P("row", "col", None),
        check_vma=False,
    )
```

```python
import jax
import jax.numpy as jnp
from jax import lax
from jax.experimental import pallas as pl
from jax.experimental.pallas import tpu as pltpu
from jax.sharding import PartitionSpec as P


MESH = pl.DeviceIdType.MESH
TOK = 40
ROWS = 16
PLANE = 8
CHIPS = ROWS * PLANE
CH = 128
PERM = 16 * 128
BF = jnp.bfloat16
F32 = jnp.float32
VMEM_LIMIT = 40 * 2**20


def sigmoid(x):
    return 0.5 * jnp.tanh(0.5 * x) + 0.5


def norm_lanes(x):
    center = x - jnp.mean(x, axis=-1, keepdims=True)
    spread = jnp.mean(center * center, axis=-1, keepdims=True)
    return center * lax.rsqrt(spread + 1e-05)


def start_field(pair_ref, chain_rows_ref, chain_cols_ref, bias_ref, field_ref):
    bias = bias_ref[...]
    cols = chain_cols_ref[...]
    for i in range(TOK):
        same = cols == chain_rows_ref[i]
        field_ref[pl.ds(i * TOK, TOK)] = pair_ref[i].astype(F32) + jnp.where(same, bias, 0.0)


def arrange(field_ref, nat, perm, swap):
    nat[...] = norm_lanes(field_ref[...])
    for g in range(16):
        for q in range(3):
            a = 16 * q + g
            at = pl.ds(g * 128 + TOK * q, TOK)
            if a >= TOK:
                perm[at] = jnp.zeros((TOK, CH), F32)
            elif swap:
                perm[at] = nat[pl.ds(a, TOK, stride=TOK)]
            else:
                perm[at] = nat[pl.ds(a * TOK, TOK)]
        perm[pl.ds(g * 128 + 120, 8)] = jnp.zeros((8, CH), F32)


def project(perm, w, mask, out, tiles):
    weights_t = jnp.transpose(w.astype(F32)).astype(BF)
    for part in range(4):
        normed = perm[pl.ds(part * 512, 512)].astype(BF)
        both = lax.dot_general(weights_t, normed, (((1,), (1,)), ((), ())), preferred_element_type=F32)
        value = sigmoid(both[:CH]) * both[CH:]
        for n in range(4):
            g = part * 4 + n
            tiles[pl.ds(g, CH, stride=16)] = value[:, n * 128 : n * 128 + 128] * mask[g : g + 1, :]
    out[...] = tiles[...].reshape(CH, 16, 128).astype(BF)


def project_gate(perm, w, gate_ref, swap):
    for part in range(4):
        normed = perm[pl.ds(part * 512, 512)].astype(BF)
        value = sigmoid(jnp.dot(normed, w, preferred_element_type=F32))
        for n in range(4):
            for q in range(3):
                a = 16 * q + part * 4 + n
                if a < TOK:
                    piece = value[n * 128 + q * TOK : n * 128 + q * TOK + TOK]
                    if swap:
                        gate_ref[pl.ds(a, TOK, stride=TOK)] = piece
                    else:
                        gate_ref[pl.ds(a * TOK, TOK)] = piece


def finish(field_ref, gate_ref, r_ref, weights, tiles):
    x = r_ref[...].astype(F32)
    center = x - jnp.mean(x, axis=0, keepdims=True)
    spread = jnp.mean(center * center, axis=0, keepdims=True)
    tiles[...] = (center * lax.rsqrt(spread + 1e-05)).reshape(CH * 16, 128)
    for g in range(16):
        normed = tiles[pl.ds(g, CH, stride=16)].astype(BF)
        out = lax.dot_general(normed, weights, (((0,), (0,)), ((), ())), preferred_element_type=F32)
        for q in range(3):
            a = 16 * q + g
            if a < TOK:
                at = pl.ds(a * TOK, TOK)
                field_ref[at] = field_ref[at] + gate_ref[at] * out[q * TOK : q * TOK + TOK]


def lanes_between(lo, hi, rows):
    lane = lax.broadcasted_iota(jnp.int32, (rows, 128), 1)
    return (lane >= lo) & (lane < hi)


def roll(x, amount):
    amount = amount % 128
    return pltpu.roll(x, amount, 1) if amount else x


def spread_lanes(blocks, q, rows):
    total = jnp.zeros((rows, 128), F32)
    for m, block in enumerate(blocks):
        total = jnp.where(lanes_between(TOK * m, TOK * m + TOK, rows), roll(block, TOK * (m - q)), total)
    return total


def triangle(load_m, load_n, out_ref, left, right, part):
    part[...] = jnp.zeros((384, 128), F32)
    for group in range(6):
        blocks = range(3 * group, min(3 * group + 3, 16))
        lane = pl.ds(group * 128, 128)
        m_blocks = [load_m(k).astype(F32) for k in blocks]
        n_blocks = [load_n(k).astype(F32) for k in blocks]
        for q in range(3):
            left[pl.ds(q * 256, 256), lane] = spread_lanes(m_blocks, q, 256).astype(BF)
            value = spread_lanes(n_blocks, q, 128)
            for n in range(8):
                depth = 16 if q < 2 else 8
                part[pl.ds(128 * (n // 3) + TOK * (n % 3) + 16 * q, depth)] = value[n * 16 : n * 16 + depth]
        right[:, lane] = part[...].astype(BF)
    for n3 in range(3):
        total = lax.dot_general(
            left[...], right[pl.ds(n3 * 128, 128)], (((1,), (1,)), ((), ())), preferred_element_type=F32
        )
        for m in range(3 if n3 < 2 else 2):
            value = jnp.zeros((256, 128), F32)
            for q in range(3):
                value = jnp.where(
                    lanes_between(TOK * q, TOK * q + TOK, 256),
                    roll(total[q * 256 : q * 256 + 256], TOK * (q - m)),
                    value,
                )
            out_ref[3 * n3 + m] = value.reshape(16, 16, 128).astype(BF)


def place():
    row, col = lax.axis_index("row"), lax.axis_index("col")
    return row, col // 2, col % 2


def each_chip(visit):
    row, chip, core = place()
    rows = [row] + [(row + step) % ROWS for step in range(1, ROWS)]
    for to_row in rows[1:]:
        visit(to_row, chip)

    def column(step, carry):
        to_chip = (chip + step) % PLANE
        for to_row in rows:
            visit(to_row, to_chip)
        return carry

    lax.fori_loop(1, PLANE, column, 0)


def greet():
    row, chip, core = place()
    barrier = pltpu.get_barrier_semaphore()

    def signal(to_row, to_chip):
        pl.semaphore_signal(barrier, inc=1, device_id=(to_row, to_chip * 2 + core), device_id_type=MESH)

    each_chip(signal)
    pl.semaphore_signal(barrier, inc=1, device_id=(row, chip * 2 + 1 - core), device_id_type=MESH)


def send_all(src, dst, send_sem, recv_sem):
    row, chip, core = place()

    def send(to_row, to_chip):
        pltpu.make_async_remote_copy(
            src_ref=src(to_row, to_chip),
            dst_ref=dst,
            send_sem=send_sem,
            recv_sem=recv_sem,
            device_id=(to_row, to_chip * 2 + core),
            device_id_type=MESH,
        ).start()

    each_chip(send)
    pltpu.make_async_copy(src(row, chip), dst, recv_sem).start()


def wait_bytes(ref, sem):
    pltpu.make_async_copy(ref, ref, sem).wait()


def to_sibling(ref, send_sem, recv_sem):
    row, chip, core = place()
    copy = pltpu.make_async_remote_copy(
        src_ref=ref,
        dst_ref=ref,
        send_sem=send_sem,
        recv_sem=recv_sem,
        device_id=(row, chip * 2 + 1 - core),
        device_id_type=MESH,
    )
    copy.start()
    return copy


def kernel(
    pair_ref, rows_ref, cols_ref, bias_ref, w_ref, wo_ref, mask_ref, out_ref,
    field, gate, nat, perm, tiles, f_ref, s_ref, o_ref, rf_out, rs_out, rf_in, rs_in, back_out, back_in,
    left, right, part, send_sem, recv_sem, on_send, on_recv,
):
    row, chip, core = place()
    index = row * PLANE + chip
    some = f_ref.at[pl.ds(0, CHIPS - 1)]
    greet()

    start_field(pair_ref, rows_ref, cols_ref, bias_ref, field)
    arrange(field, nat, perm, False)
    project(perm, w_ref[0, :, :256], mask_ref[0], f_ref, tiles)
    pl.semaphore_wait(pltpu.get_barrier_semaphore(), CHIPS)
    send_all(lambda r, c: f_ref.at[r * PLANE + c], rf_out.at[core, chip, row], send_sem.at[0], recv_sem.at[0])
    project(perm, w_ref[0, :, 256:512], mask_ref[0], s_ref, tiles)
    send_all(
        lambda r, c: s_ref.at[r * PLANE + c],
        rs_out.at[row % 2, core, chip, row // 2],
        send_sem.at[1],
        recv_sem.at[1 + row % 2],
    )
    project_gate(perm, w_ref[0, :, 512:], gate, False)
    wait_bytes(rf_out.at[0], recv_sem.at[0])
    copy_f = to_sibling(rf_out.at[core], on_send.at[0], on_recv.at[0])
    wait_bytes(rs_out.at[0, 0], recv_sem.at[2 - core])
    copy_s = to_sibling(rs_out.at[1 - core, core], on_send.at[1], on_recv.at[1])
    wait_bytes(rs_out.at[0, 0], recv_sem.at[1 + core])
    copy_f.wait()
    copy_s.wait()
    wait_bytes(some, send_sem.at[0])
    wait_bytes(some, send_sem.at[1])
    triangle(
        lambda k: rf_out[k % 2, k // 2].reshape(256, 128),
        lambda k: rs_out[core, k % 2, k // 2].reshape(128, 128),
        o_ref,
        left,
        right,
        part,
    )
    send_all(lambda r, c: o_ref.at[c, r], back_out.at[index], send_sem.at[2], recv_sem.at[3])
    wait_bytes(back_out, recv_sem.at[3])
    wait_bytes(some, send_sem.at[2])
    finish(field, gate, back_out, wo_ref[0], tiles)

    arrange(field, nat, perm, True)
    project(perm, w_ref[1, :, :256], mask_ref[1], f_ref, tiles)
    send_all(lambda r, c: f_ref.at[r * PLANE + c], rf_in.at[core, row, chip], send_sem.at[3], recv_sem.at[4])
    project(perm, w_ref[1, :, 256:512], mask_ref[1], s_ref, tiles)
    send_all(lambda r, c: s_ref.at[r * PLANE + c], rs_in.at[row, chip], send_sem.at[4], recv_sem.at[5])
    project_gate(perm, w_ref[1, :, 512:], gate, True)
    wait_bytes(rf_in.at[0], recv_sem.at[4])
    copy_f = to_sibling(rf_in.at[core], on_send.at[2], on_recv.at[2])
    wait_bytes(rs_in, recv_sem.at[5])
    copy_f.wait()
    wait_bytes(some, send_sem.at[3])
    wait_bytes(some, send_sem.at[4])
    triangle(
        lambda k: jnp.concatenate([rf_in[0, k], rf_in[1, k]], axis=0).reshape(256, 128),
        lambda k: rs_in[k].reshape(128, 128),
        o_ref,
        left,
        right,
        part,
    )
    send_all(
        lambda r, c: o_ref.at[c, (r % 2) * PLANE + r // 2], back_in.at[index], send_sem.at[5], recv_sem.at[6]
    )
    wait_bytes(back_in, recv_sem.at[6])
    wait_bytes(some, send_sem.at[5])
    finish(field, gate, back_in, wo_ref[1], tiles)
    for i in range(TOK):
        out_ref[i] = field[pl.ds(i * TOK, TOK)].astype(BF)


def tile_mask(a_valid, b_valid):
    a = jnp.pad(a_valid, (0, 8)).reshape(3, 16).T
    return jnp.pad((a[:, :, None] * b_valid[None, None, :]).reshape(16, 120), ((0, 0), (0, 8)))


def per_device(pair, token_mask, chain_ids, chain_bias, in_weights, out_weights):
    row_start = lax.axis_index("row") * TOK
    col_start = lax.axis_index("col") * TOK
    valid_rows = lax.dynamic_slice_in_dim(token_mask, row_start, TOK).astype(F32)
    valid_cols = lax.dynamic_slice_in_dim(token_mask, col_start, TOK).astype(F32)
    chain_rows = lax.dynamic_slice_in_dim(chain_ids, row_start, TOK)
    chain_cols = lax.dynamic_slice_in_dim(chain_ids, col_start, TOK)
    masks = jnp.stack([tile_mask(valid_rows, valid_cols), tile_mask(valid_cols, valid_rows)])
    chain_cols = jnp.broadcast_to(chain_cols[:, None], (TOK, CH))
    vmem = pl.BlockSpec(memory_space=pltpu.VMEM)
    dma = pltpu.SemaphoreType.DMA
    return pl.pallas_call(
        kernel,
        out_shape=jax.ShapeDtypeStruct((TOK, TOK, CH), BF),
        in_specs=[vmem, pl.BlockSpec(memory_space=pltpu.SMEM)] + [vmem] * 5,
        out_specs=vmem,
        scratch_shapes=[
            pltpu.VMEM((TOK * TOK, CH), F32),
            pltpu.VMEM((TOK * TOK, CH), F32),
            pltpu.VMEM((TOK * TOK, CH), F32),
            pltpu.VMEM((PERM, CH), F32),
            pltpu.VMEM((PERM, CH), F32),
            pltpu.VMEM((CH, 16, 128), BF),
            pltpu.VMEM((CH, 16, 128), BF),
            pltpu.VMEM((8, 16, 16, 128), BF),
            pltpu.VMEM((2, 8, 16, 16, 128), BF),
            pltpu.VMEM((2, 2, 8, 8, 16, 128), BF),
            pltpu.VMEM((2, 16, 8, 16, 128), BF),
            pltpu.VMEM((16, 8, 16, 128), BF),
            pltpu.VMEM((CH, 16, 128), BF),
            pltpu.VMEM((CH, 16, 128), BF),
            pltpu.VMEM((768, 768), BF),
            pltpu.VMEM((384, 768), BF),
            pltpu.VMEM((384, 128), F32),
            dma((6,)),
            dma((7,)),
            dma((3,)),
            dma((3,)),
        ],
        compiler_params=pltpu.CompilerParams(
            collective_id=0, has_side_effects=True, vmem_limit_bytes=VMEM_LIMIT
        ),
        cost_estimate=pl.CostEstimate(flops=10**9, bytes_accessed=2 * 10**6, transcendentals=10**6),
        name="pairformer",
    )(pair, chain_rows, chain_cols, chain_bias.reshape(1, CH), in_weights, out_weights, masks)


def solution(mesh):
    return jax.shard_map(
        per_device,
        mesh=mesh,
        in_specs=(P("row", "col", None), P(), P(), P(), P(), P()),
        out_specs=P("row", "col", None),
        check_vma=False,
    )
```

```python
import jax
import jax.numpy as jnp
from jax import lax
from jax.experimental import pallas as pl
from jax.experimental.pallas import tpu as pltpu
from jax.sharding import PartitionSpec as P


MESH = pl.DeviceIdType.MESH
TOK = 40
ROWS = 16
PLANE = 8
CHIPS = ROWS * PLANE
CH = 128
PERM = 16 * 128
BF = jnp.bfloat16
F32 = jnp.float32
VMEM_LIMIT = 60 * 2**20
STEPS_X = (2, 1, 3, 0)
STEPS_Y = (2, 1, 3, 0)
STEPS_Z = (4, 0, 3, 5, 1, 7, 2, 6)


def sigmoid(x):
    return 0.5 * jnp.tanh(0.5 * x) + 0.5


def norm_lanes(x):
    center = x - jnp.mean(x, axis=-1, keepdims=True)
    spread = jnp.mean(center * center, axis=-1, keepdims=True)
    return center * lax.rsqrt(spread + 1e-05)


def start_field(pair_ref, ids_ref, bias_ref, field_ref, column):
    row, col = lax.axis_index("row"), lax.axis_index("col")
    for j in range(TOK):
        column[j : j + 1, :] = jnp.full((1, CH), ids_ref[col * TOK + j], jnp.int32)
    bias = bias_ref[...]
    cols = column[...]
    for i in range(TOK):
        same = cols == ids_ref[row * TOK + i]
        field_ref[pl.ds(i * TOK, TOK)] = pair_ref[i].astype(F32) + jnp.where(same, bias, 0.0)


def tile_masks(valid_ref, mask):
    row, col = lax.axis_index("row"), lax.axis_index("col")
    lane = lax.broadcasted_iota(jnp.int32, (1, 128), 1)
    third = (lane >= TOK).astype(jnp.int32) + (lane >= 2 * TOK).astype(jnp.int32)
    place_b = jnp.where(lane < 3 * TOK, lane - TOK * third, TOK)
    rows = [valid_ref[row * TOK + n].astype(F32) for n in range(TOK)]
    cols = [valid_ref[col * TOK + n].astype(F32) for n in range(TOK)]
    for d, (a_valid, b_valid) in enumerate(((rows, cols), (cols, rows))):
        along = jnp.zeros((1, 128), F32)
        for b in range(TOK):
            along = jnp.where(place_b == b, b_valid[b], along)
        for g in range(16):
            low = jnp.where(third == 0, a_valid[g], a_valid[16 + g])
            high = a_valid[32 + g] if 32 + g < TOK else 0.0
            mask[d, g : g + 1, :] = jnp.where(third == 2, high, low) * along


def arrange(field_ref, nat, perm, swap):
    nat[...] = norm_lanes(field_ref[...])
    for g in range(16):
        for q in range(3):
            a = 16 * q + g
            at = pl.ds(g * 128 + TOK * q, TOK)
            if a >= TOK:
                perm[at] = jnp.zeros((TOK, CH), F32)
            elif swap:
                perm[at] = nat[pl.ds(a, TOK, stride=TOK)]
            else:
                perm[at] = nat[pl.ds(a * TOK, TOK)]
        perm[pl.ds(g * 128 + 120, 8)] = jnp.zeros((8, CH), F32)


def project(perm, w, mask, out, tiles):
    weights_t = jnp.transpose(w.astype(F32)).astype(BF)
    for part in range(4):
        normed = perm[pl.ds(part * 512, 512)].astype(BF)
        both = lax.dot_general(weights_t, normed, (((1,), (1,)), ((), ())), preferred_element_type=F32)
        value = sigmoid(both[:CH]) * both[CH:]
        for n in range(4):
            g = part * 4 + n
            tiles[pl.ds(g, CH, stride=16)] = value[:, n * 128 : n * 128 + 128] * mask[g : g + 1, :]
    out[...] = tiles[...].reshape(CH, 16, 128).astype(BF)


def project_gate(perm, w, gate_ref, swap):
    for part in range(4):
        normed = perm[pl.ds(part * 512, 512)].astype(BF)
        value = sigmoid(jnp.dot(normed, w, preferred_element_type=F32))
        for n in range(4):
            for q in range(3):
                a = 16 * q + part * 4 + n
                if a < TOK:
                    piece = value[n * 128 + q * TOK : n * 128 + q * TOK + TOK]
                    if swap:
                        gate_ref[pl.ds(a, TOK, stride=TOK)] = piece
                    else:
                        gate_ref[pl.ds(a * TOK, TOK)] = piece


def finish(field_ref, gate_ref, r_ref, weights, tiles):
    x = r_ref[...].astype(F32)
    center = x - jnp.mean(x, axis=0, keepdims=True)
    spread = jnp.mean(center * center, axis=0, keepdims=True)
    tiles[...] = (center * lax.rsqrt(spread + 1e-05)).reshape(CH * 16, 128)
    for g in range(16):
        normed = tiles[pl.ds(g, CH, stride=16)].astype(BF)
        out = lax.dot_general(normed, weights, (((0,), (0,)), ((), ())), preferred_element_type=F32)
        for q in range(3):
            a = 16 * q + g
            if a < TOK:
                at = pl.ds(a * TOK, TOK)
                field_ref[at] = field_ref[at] + gate_ref[at] * out[q * TOK : q * TOK + TOK]


def lanes_between(lo, hi, rows):
    lane = lax.broadcasted_iota(jnp.int32, (rows, 128), 1)
    return (lane >= lo) & (lane < hi)


def roll(x, amount):
    amount = amount % 128
    return pltpu.roll(x, amount, 1) if amount else x


def spread_lanes(blocks, q, rows):
    total = jnp.zeros((rows, 128), F32)
    for m, block in enumerate(blocks):
        total = jnp.where(lanes_between(TOK * m, TOK * m + TOK, rows), roll(block, TOK * (m - q)), total)
    return total


def assemble(load_m, load_n, left, right, part):
    part[...] = jnp.zeros((384, 128), F32)
    for group in range(6):
        blocks = range(3 * group, min(3 * group + 3, 16))
        lane = pl.ds(group * 128, 128)
        m_blocks = [load_m(k).astype(F32) for k in blocks]
        n_blocks = [load_n(k).astype(F32) for k in blocks]
        for q in range(3):
            left[pl.ds(q * 256, 256), lane] = spread_lanes(m_blocks, q, 256).astype(BF)
            value = spread_lanes(n_blocks, q, 128)
            for n in range(8):
                depth = 16 if q < 2 else 8
                part[pl.ds(128 * (n // 3) + TOK * (n % 3) + 16 * q, depth)] = value[n * 16 : n * 16 + depth]
        right[:, lane] = part[...].astype(BF)


def multiply(x_to, left, right, out_ref):
    rows = [left[pl.ds(pl.multiple_of(q * 256 + x_to * 64, 64), 64)] for q in range(3)]
    total = lax.dot_general(
        jnp.concatenate(rows, axis=0), right[...], (((1,), (1,)), ((), ())), preferred_element_type=F32
    )
    for n in range(8):
        n3, m = n // 3, n % 3
        value = jnp.zeros((64, 128), F32)
        for q in range(3):
            value = jnp.where(
                lanes_between(TOK * q, TOK * q + TOK, 64),
                roll(total[q * 64 : q * 64 + 64, n3 * 128 : n3 * 128 + 128], TOK * (q - m)),
                value,
            )
        out_ref[n, pl.ds(x_to * 4, 4)] = value.reshape(4, 16, 128).astype(BF)


def place():
    row, col = lax.axis_index("row"), lax.axis_index("col")
    return row, col // 2, col % 2


def greet(line):
    row, chip, core = place()
    barrier = pltpu.get_barrier_semaphore()
    chips = [(chip + step) % PLANE for step in range(1, PLANE)]
    for step in range(1, ROWS):
        pl.semaphore_signal(
            barrier, inc=1, device_id=((row + step) % ROWS, chip * 2 + core), device_id_type=MESH
        )
    for to_chip in chips:
        pl.semaphore_signal(barrier, inc=1, device_id=(row, to_chip * 2 + core), device_id_type=MESH)
    pl.semaphore_signal(barrier, inc=1, device_id=(row, chip * 2 + 1 - core), device_id_type=MESH)

    def arrived():
        pl.semaphore_wait(barrier, ROWS + PLANE - 1)
        for to_chip in chips:
            pl.semaphore_signal(line, inc=1, device_id=(row, to_chip * 2 + core), device_id_type=MESH)

    return arrived


class Offsets:
    def __init__(self):
        self.row, self.chip, self.core = place()
        x, y, z = self.row // 4, self.chip // 2, self.row % 4 * 2 + self.chip % 2
        self.x = [x] + [(x + step) % 4 for step in range(1, 4)]
        y = [y] + [(y + step) % 4 for step in range(1, 4)]
        z = [z] + [(z + step) % 8 for step in range(1, 8)]
        self.y = [value * 2 for value in y]
        self.z = [(value // 2, value % 2) for value in z]

    def at(self, dx, dy, dz):
        return self.x[dx] * 4 + self.z[dz][0], self.y[dy] + self.z[dz][1]

    def send(self, dx, arrays):
        for dy in STEPS_Y:
            for dz in STEPS_Z:
                to_row, to_chip = self.at(dx, dy, dz)
                for src, dst, send_sem, recv_sem in arrays:
                    if (dx, dy, dz) == (0, 0, 0):
                        pltpu.make_async_copy(src(self.row, self.chip), dst, recv_sem).start()
                    else:
                        pltpu.make_async_remote_copy(
                            src_ref=src(to_row, to_chip),
                            dst_ref=dst,
                            send_sem=send_sem,
                            recv_sem=recv_sem,
                            device_id=(to_row, to_chip * 2 + self.core),
                            device_id_type=MESH,
                        ).start()


def wait_bytes(ref, sem):
    pltpu.make_async_copy(ref, ref, sem).wait()


def to_sibling(ref, send_sem, recv_sem):
    row, chip, core = place()
    copy = pltpu.make_async_remote_copy(
        src_ref=ref,
        dst_ref=ref,
        send_sem=send_sem,
        recv_sem=recv_sem,
        device_id=(row, chip * 2 + 1 - core),
        device_id_type=MESH,
    )
    copy.start()
    return copy


def kernel(
    pair_hbm, valid_ref, ids_ref, bias_ref, w_hbm, wo_hbm, out_ref,
    pair_ref, w_ref, wo_ref, mask_ref, column, field, gate, nat, perm, tiles, f_ref, s_ref, o_ref,
    rf_out, rs_out, rf_in, rs_in, back_out, back_in, left, right, part,
    load_sem, line, send_sem, f_recv, s_recv, s_in_recv, back_recv, on_send, on_recv,
):
    row, chip, core = place()
    index = row * PLANE + chip
    some = f_ref.at[pl.ds(0, CHIPS - 1)]
    loads = [
        pltpu.make_async_copy(src, dst, load_sem.at[n])
        for n, (src, dst) in enumerate(((pair_hbm, pair_ref), (w_hbm, w_ref), (wo_hbm, wo_ref)))
    ]
    for load in loads:
        load.start()
    arrived = greet(line)
    offsets = Offsets()

    tile_masks(valid_ref, mask_ref)
    loads[0].wait()
    start_field(pair_ref, ids_ref, bias_ref, field, column)
    arrange(field, nat, perm, False)
    arrived()
    loads[1].wait()
    project(perm, w_ref[0, :, :256], mask_ref[0], f_ref, tiles)
    project(perm, w_ref[0, :, 256:512], mask_ref[0], s_ref, tiles)
    pl.semaphore_wait(line, PLANE - 1)
    parity = row % 2
    for dx in STEPS_X:
        offsets.send(
            dx,
            [
                (lambda r, c: f_ref.at[r * PLANE + c], rf_out.at[core, chip, row], send_sem.at[0], f_recv.at[dx]),
                (
                    lambda r, c: s_ref.at[r * PLANE + c],
                    rs_out.at[parity, core, chip, row // 2],
                    send_sem.at[1],
                    s_recv.at[parity * 4 + dx],
                ),
            ],
        )
    project_gate(perm, w_ref[0, :, 512:], gate, False)
    loads[2].wait()
    copies = []
    for dx in STEPS_X:
        x_from = offsets.x[-dx % 4]
        whole = rf_out.at[core, :, pl.ds(x_from * 4, 4)]
        wait_bytes(whole, f_recv.at[dx])
        copies.append(to_sibling(whole, on_send.at[dx], on_recv.at[dx]))
        half = rs_out.at[1 - core, core, :, pl.ds(x_from * 2, 2)]
        wait_bytes(half, s_recv.at[(1 - core) * 4 + dx])
        copies.append(to_sibling(half, on_send.at[4 + dx], on_recv.at[4 + dx]))
    for dx in STEPS_X:
        wait_bytes(rs_out.at[core, core, :, pl.ds(offsets.x[-dx % 4] * 2, 2)], s_recv.at[core * 4 + dx])
    for copy in copies:
        copy.wait()
    assemble(
        lambda k: rf_out[k % 2, k // 2].reshape(256, 128),
        lambda k: rs_out[core, k % 2, k // 2].reshape(128, 128),
        left,
        right,
        part,
    )
    for dx in STEPS_X:
        multiply(offsets.x[dx], left, right, o_ref)
        offsets.send(dx, [(lambda r, c: o_ref.at[c, r], back_out.at[index], send_sem.at[2], back_recv.at[0])])
    wait_bytes(some, send_sem.at[0])
    wait_bytes(some, send_sem.at[1])
    wait_bytes(back_out, back_recv.at[0])
    wait_bytes(some, send_sem.at[2])
    finish(field, gate, back_out, wo_ref[0], tiles)

    arrange(field, nat, perm, True)
    project(perm, w_ref[1, :, :256], mask_ref[1], f_ref, tiles)
    project(perm, w_ref[1, :, 256:512], mask_ref[1], s_ref, tiles)
    for dx in STEPS_X:
        offsets.send(
            dx,
            [
                (lambda r, c: f_ref.at[r * PLANE + c], rf_in.at[core, row, chip], send_sem.at[3], f_recv.at[4 + dx]),
                (lambda r, c: s_ref.at[r * PLANE + c], rs_in.at[row, chip], send_sem.at[4], s_in_recv),
            ],
        )
    project_gate(perm, w_ref[1, :, 512:], gate, True)
    copies = []
    for dx in STEPS_X:
        whole = rf_in.at[core, pl.ds(offsets.x[-dx % 4] * 4, 4)]
        wait_bytes(whole, f_recv.at[4 + dx])
        copies.append(to_sibling(whole, on_send.at[8 + dx], on_recv.at[8 + dx]))
    wait_bytes(rs_in, s_in_recv)
    for copy in copies:
        copy.wait()
    assemble(
        lambda k: jnp.concatenate([rf_in[n % 2, k, n // 2] for n in range(16)], axis=0),
        lambda k: rs_in[k].reshape(128, 128),
        left,
        right,
        part,
    )
    for dx in STEPS_X:
        multiply(offsets.x[dx], left, right, o_ref)
        offsets.send(dx, [(lambda r, c: o_ref.at[c, r], back_in.at[index], send_sem.at[5], back_recv.at[1])])
    wait_bytes(some, send_sem.at[3])
    wait_bytes(some, send_sem.at[4])
    wait_bytes(back_in, back_recv.at[1])
    wait_bytes(some, send_sem.at[5])
    finish(field, gate, back_in, wo_ref[1], tiles)
    for i in range(TOK):
        out_ref[i] = field[pl.ds(i * TOK, TOK)].astype(BF)


def per_device(pair, token_mask, chain_ids, chain_bias, in_weights, out_weights):
    hbm = pl.BlockSpec(memory_space=pl.ANY)
    smem = pl.BlockSpec(memory_space=pltpu.SMEM)
    vmem = pl.BlockSpec(memory_space=pltpu.VMEM)
    dma = pltpu.SemaphoreType.DMA
    tokens = pltpu.VMEM((TOK * TOK, CH), F32)
    return pl.pallas_call(
        kernel,
        out_shape=jax.ShapeDtypeStruct((TOK, TOK, CH), BF),
        in_specs=[hbm, smem, smem, vmem, hbm, hbm],
        out_specs=vmem,
        scratch_shapes=[
            pltpu.VMEM((TOK, TOK, CH), BF),
            pltpu.VMEM((2, CH, 5 * CH), BF),
            pltpu.VMEM((2, CH, CH), BF),
            pltpu.VMEM((2, 16, 128), F32),
            pltpu.VMEM((TOK, CH), jnp.int32),
            tokens,
            tokens,
            tokens,
            pltpu.VMEM((PERM, CH), F32),
            pltpu.VMEM((PERM, CH), F32),
            pltpu.VMEM((CH, 16, 128), BF),
            pltpu.VMEM((CH, 16, 128), BF),
            pltpu.VMEM((8, 16, 16, 128), BF),
            pltpu.VMEM((2, 8, 16, 16, 128), BF),
            pltpu.VMEM((2, 2, 8, 8, 16, 128), BF),
            pltpu.VMEM((2, 16, 8, 16, 128), BF),
            pltpu.VMEM((16, 8, 16, 128), BF),
            pltpu.VMEM((CH, 16, 128), BF),
            pltpu.VMEM((CH, 16, 128), BF),
            pltpu.VMEM((768, 768), BF),
            pltpu.VMEM((384, 768), BF),
            pltpu.VMEM((384, 128), F32),
            dma((3,)),
            pltpu.SemaphoreType.REGULAR,
            dma((6,)),
            dma((8,)),
            dma((8,)),
            dma,
            dma((2,)),
            dma((12,)),
            dma((12,)),
        ],
        compiler_params=pltpu.CompilerParams(
            collective_id=0, has_side_effects=True, vmem_limit_bytes=VMEM_LIMIT
        ),
        cost_estimate=pl.CostEstimate(flops=10**9, bytes_accessed=2 * 10**6, transcendentals=10**6),
        name="pairformer",
    )(pair, token_mask, chain_ids, chain_bias.reshape(1, CH), in_weights, out_weights)


def solution(mesh):
    return jax.shard_map(
        per_device,
        mesh=mesh,
        in_specs=(P("row", "col", None), P(), P(), P(), P(), P()),
        out_specs=P("row", "col", None),
        check_vma=False,
    )
```

```python
import jax
import jax.numpy as jnp
from jax import lax
from jax.experimental import pallas as pl
from jax.experimental.pallas import tpu as pltpu
from jax.sharding import PartitionSpec as P


MESH = pl.DeviceIdType.MESH
TOK = 40
ROWS = 16
PLANE = 8
CHIPS = ROWS * PLANE
CH = 128
PERM = 16 * 128
BF = jnp.bfloat16
F32 = jnp.float32
VMEM_LIMIT = 60 * 2**20
STEPS_Y = (2, 1, 3, 0)
STEPS_Z = (4, 0, 3, 5, 1, 7, 2, 6)
GROUPS = ((0, 1, 2), (3, 4, 5), (6, 7), (8, 9, 10), (11, 12, 13), (14, 15))


def sigmoid(x):
    return 0.5 * jnp.tanh(0.5 * x) + 0.5


def norm_lanes(x):
    center = x - jnp.mean(x, axis=-1, keepdims=True)
    spread = jnp.mean(center * center, axis=-1, keepdims=True)
    return center * lax.rsqrt(spread + 1e-05)


def start_field(pair_ref, ids_ref, bias_ref, field_ref, column):
    row, col = lax.axis_index("row"), lax.axis_index("col")
    for j in range(TOK):
        column[j : j + 1, :] = jnp.full((1, CH), ids_ref[col * TOK + j], jnp.int32)
    bias = bias_ref[...]
    cols = column[...]
    for i in range(TOK):
        same = cols == ids_ref[row * TOK + i]
        field_ref[pl.ds(i * TOK, TOK)] = pair_ref[i].astype(F32) + jnp.where(same, bias, 0.0)


def tile_masks(valid_ref, mask):
    row, col = lax.axis_index("row"), lax.axis_index("col")
    lane = lax.broadcasted_iota(jnp.int32, (1, 128), 1)
    third = (lane >= TOK).astype(jnp.int32) + (lane >= 2 * TOK).astype(jnp.int32)
    place_b = jnp.where(lane < 3 * TOK, lane - TOK * third, TOK)
    rows = [valid_ref[row * TOK + n].astype(F32) for n in range(TOK)]
    cols = [valid_ref[col * TOK + n].astype(F32) for n in range(TOK)]
    for d, (a_valid, b_valid) in enumerate(((rows, cols), (cols, rows))):
        along = jnp.zeros((1, 128), F32)
        for b in range(TOK):
            along = jnp.where(place_b == b, b_valid[b], along)
        for g in range(16):
            low = jnp.where(third == 0, a_valid[g], a_valid[16 + g])
            high = a_valid[32 + g] if 32 + g < TOK else 0.0
            mask[d, g : g + 1, :] = jnp.where(third == 2, high, low) * along


def arrange(field_ref, nat, perm, swap):
    nat[...] = norm_lanes(field_ref[...])
    for g in range(16):
        for q in range(3):
            a = 16 * q + g
            at = pl.ds(g * 128 + TOK * q, TOK)
            if a >= TOK:
                perm[at] = jnp.zeros((TOK, CH), F32)
            elif swap:
                perm[at] = nat[pl.ds(a, TOK, stride=TOK)]
            else:
                perm[at] = nat[pl.ds(a * TOK, TOK)]
        perm[pl.ds(g * 128 + 120, 8)] = jnp.zeros((8, CH), F32)


def project(perm, w, mask, tiles):
    weights_t = jnp.transpose(w.astype(F32)).astype(BF)
    for part in range(4):
        normed = perm[pl.ds(part * 512, 512)].astype(BF)
        both = lax.dot_general(weights_t, normed, (((1,), (1,)), ((), ())), preferred_element_type=F32)
        value = sigmoid(both[:CH]) * both[CH:]
        for n in range(4):
            g = part * 4 + n
            tiles[pl.ds(g, CH, stride=16)] = value[:, n * 128 : n * 128 + 128] * mask[g : g + 1, :]
    return tiles[...].reshape(CH, 2, 8, 128).astype(BF)


def project_gate(perm, w, gate_ref, swap):
    for part in range(4):
        normed = perm[pl.ds(part * 512, 512)].astype(BF)
        value = sigmoid(jnp.dot(normed, w, preferred_element_type=F32))
        for n in range(4):
            for q in range(3):
                a = 16 * q + part * 4 + n
                if a < TOK:
                    piece = value[n * 128 + q * TOK : n * 128 + q * TOK + TOK]
                    if swap:
                        gate_ref[pl.ds(a, TOK, stride=TOK)] = piece
                    else:
                        gate_ref[pl.ds(a * TOK, TOK)] = piece


def finish(field_ref, gate_ref, r_ref, weights, tiles, half):
    x = r_ref[...].astype(F32)
    center = x - jnp.mean(x, axis=0, keepdims=True)
    spread = jnp.mean(center * center, axis=0, keepdims=True)
    tiles[pl.ds(0, CH * 8)] = (center * lax.rsqrt(spread + 1e-05)).reshape(CH * 8, 128)
    for g in range(8):
        normed = tiles[pl.ds(g, CH, stride=8)].astype(BF)
        out = lax.dot_general(normed, weights, (((0,), (0,)), ((), ())), preferred_element_type=F32)
        for q in range(3 - half):
            a = 16 * q + 8 * half + g
            at = pl.ds(a * TOK, TOK)
            field_ref[at] = field_ref[at] + gate_ref[at] * out[q * TOK : q * TOK + TOK]


def lanes_between(lo, hi, rows):
    lane = lax.broadcasted_iota(jnp.int32, (rows, 128), 1)
    return (lane >= lo) & (lane < hi)


def roll(x, amount):
    amount = amount % 128
    return pltpu.roll(x, amount, 1) if amount else x


def spread_lanes(blocks, q, rows):
    total = jnp.zeros((rows, 128), F32)
    for m, block in enumerate(blocks):
        total = jnp.where(lanes_between(TOK * m, TOK * m + TOK, rows), roll(block, TOK * (m - q)), total)
    return total


def assemble_right(load_n, right, part):
    part[...] = jnp.zeros((768, 128), F32)
    for group, blocks in enumerate(GROUPS):
        parts = [load_n(k).astype(F32).reshape(256, 128) for k in blocks]
        for q in range(3):
            value = spread_lanes(parts, q, 256)
            for n in range(16):
                depth = 16 if q < 2 else 8
                part[pl.ds(128 * (n // 3) + TOK * (n % 3) + 16 * q, depth)] = value[n * 16 : n * 16 + depth]
        right[:, pl.ds(group * 128, 128)] = part[...].astype(BF)


def multiply(load_m, half, left, right, out_ref):
    for group, blocks in enumerate(GROUPS):
        parts = [load_m(k).astype(F32).reshape(64, 128) for k in blocks]
        for q in range(3 - half):
            left[pl.ds(q * 64, 64), pl.ds(group * 128, 128)] = spread_lanes(parts, q, 64).astype(BF)
    rows = left[pl.ds(0, 64 * (3 - half))]
    total = lax.dot_general(rows, right[...], (((1,), (1,)), ((), ())), preferred_element_type=F32)
    for n in range(16):
        n3, m = n // 3, n % 3
        value = jnp.zeros((64, 128), F32)
        for q in range(3 - half):
            value = jnp.where(
                lanes_between(TOK * q, TOK * q + TOK, 64),
                roll(total[q * 64 : q * 64 + 64, n3 * 128 : n3 * 128 + 128], TOK * (q - m)),
                value,
            )
        out_ref[n] = value.reshape(8, 8, 128).astype(BF)


def place():
    row, col = lax.axis_index("row"), lax.axis_index("col")
    return row, col // 2, col % 2


def greet(line):
    row, chip, core = place()
    barrier = pltpu.get_barrier_semaphore()
    chips = [(chip + step) % PLANE for step in range(1, PLANE)]
    for step in range(1, ROWS):
        for other in (core, 1 - core):
            pl.semaphore_signal(
                barrier, inc=1, device_id=((row + step) % ROWS, chip * 2 + other), device_id_type=MESH
            )
    for to_chip in chips:
        pl.semaphore_signal(barrier, inc=1, device_id=(row, to_chip * 2 + core), device_id_type=MESH)
    pl.semaphore_signal(barrier, inc=1, device_id=(row, chip * 2 + 1 - core), device_id_type=MESH)

    def arrived():
        pl.semaphore_wait(barrier, 2 * (ROWS - 1) + PLANE)
        for to_chip in chips:
            pl.semaphore_signal(line, inc=1, device_id=(row, to_chip * 2 + core), device_id_type=MESH)

    return arrived


def remote(src, dst, send_sem, recv_sem, to_row, to_col):
    return pltpu.make_async_remote_copy(
        src_ref=src,
        dst_ref=dst,
        send_sem=send_sem,
        recv_sem=recv_sem,
        device_id=(to_row, to_col),
        device_id_type=MESH,
    )


class Sends:
    def __init__(self):
        self.row, self.chip, self.core = place()
        self.x, y, z_hi, z_lo = self.row // 4, self.chip // 2, self.row % 4, self.chip % 2
        z = [z_hi * 2 + z_lo] + [(z_hi * 2 + z_lo + step) % 8 for step in range(1, 8)]
        self.y = [y * 2] + [(y + step) % 4 * 2 for step in range(1, 4)]
        self.z = [(value // 2, value % 2) for value in z]
        self.z_own = [
            (self.core + 2 * ((z_hi // 2 + s) % 2), (z_lo + t) % 2) for s, t in ((1, 0), (0, 0), (1, 1), (0, 1))
        ]

    def every(self, visit):
        def along(step, carry):
            for dy in STEPS_Y:
                visit((self.x + step) % 4, dy, False)
            return carry

        lax.fori_loop(1, 4, along, 0)
        for dy in STEPS_Y:
            visit(self.x, dy, dy == 0)

    def to_chips(self, src, dst, send_sem, recv_sem, to_core):
        def visit(x, dy, line):
            for dz in STEPS_Z:
                to_row, to_chip = x * 4 + self.z[dz][0], self.y[dy] + self.z[dz][1]
                if not (line and dz == 0):
                    remote(
                        src(to_row * PLANE + to_chip), dst, send_sem, recv_sem, to_row, to_chip * 2 + to_core
                    ).start()

        self.every(visit)
        self.own(src(self.row * PLANE + self.chip), dst, send_sem, recv_sem, self.row, self.chip * 2 + to_core, to_core)

    def own(self, src, dst, send_sem, recv_sem, to_row, to_col, to_core):
        if to_core is self.core:
            pltpu.make_async_copy(src, dst, recv_sem).start()
            return

        @pl.when(to_core == self.core)
        def _():
            pltpu.make_async_copy(src, dst, recv_sem).start()

        @pl.when(to_core != self.core)
        def _():
            remote(src, dst, send_sem, recv_sem, to_row, to_col).start()

    def to_owners(self, o_ref, dst, send_sem, recv_sem):
        parity = self.row % 2

        def visit(x, dy, line):
            for n, (z_hi, z_lo) in enumerate(self.z_own):
                to_row, to_chip = x * 4 + z_hi, self.y[dy] + z_lo
                for other in (0, 1):
                    to_col = to_chip * 2 + (1 - self.core if other else self.core)
                    src = o_ref.at[to_col, to_row // 2]
                    copy = remote(src, dst, send_sem, recv_sem, to_row, to_col)
                    if line and n == 1 and not other:

                        @pl.when(parity == self.core)
                        def _():
                            pltpu.make_async_copy(src, dst, recv_sem).start()

                        @pl.when(parity != self.core)
                        def _():
                            copy.start()

                    else:
                        copy.start()

        self.every(visit)

    def sent(self, ref, send_sem, across):
        wait_bytes(ref.at[pl.ds(0, CHIPS - 1)], send_sem)
        if across:

            @pl.when(self.row % 2 != self.core)
            def _():
                wait_bytes(ref.at[0], send_sem)


def wait_bytes(ref, sem):
    pltpu.make_async_copy(ref, ref, sem).wait()


def to_sibling(ref, send_sem, recv_sem):
    row, chip, core = place()
    copy = remote(ref, ref, send_sem, recv_sem, row, chip * 2 + 1 - core)
    copy.start()
    return copy


def kernel(
    pair_hbm, valid_ref, ids_ref, bias_ref, w_hbm, wo_hbm, out_ref,
    pair_ref, w_ref, wo_ref, mask_ref, column, field, gate, nat, perm, tiles, fa, fb, s_ref, oa, ob,
    ra_out, rb_out, rs_out, ra_in, rb_in, rs_in, ba_out, bb_out, ba_in, bb_in, left, right, part,
    load_sem, line, send_sem, recv_sem, on_send, on_recv,
):
    row, chip, core = place()
    index = row * PLANE + chip
    loads = [
        pltpu.make_async_copy(src, dst, load_sem.at[n])
        for n, (src, dst) in enumerate(((pair_hbm, pair_ref), (w_hbm, w_ref), (wo_hbm, wo_ref)))
    ]
    for load in loads:
        load.start()
    arrived = greet(line)
    sends = Sends()
    tile_masks(valid_ref, mask_ref)
    loads[0].wait()
    start_field(pair_ref, ids_ref, bias_ref, field, column)

    for d in range(2):
        ra, rb, rs, ba, bb = ((ra_out, rb_out, rs_out, ba_out, bb_out), (ra_in, rb_in, rs_in, ba_in, bb_in))[d]
        sem = [(send_sem.at[5 * d + n], recv_sem.at[5 * d + n]) for n in range(5)]
        if d == 0:
            f_core, f_slot, s_slot = row % 2, (core, chip, row // 2), (core, chip, row)
        else:
            f_core, f_slot, s_slot = core, (row, chip), (core, row, chip)
        arrange(field, nat, perm, d == 1)
        if d == 0:
            arrived()
            loads[1].wait()
        s_ref[...] = project(perm, w_ref[d, :, 256:512], mask_ref[d], tiles)
        if d == 0:
            pl.semaphore_wait(line, PLANE - 1)
        sends.to_chips(lambda n: s_ref.at[n], rs.at[s_slot], *sem[0], sends.core)
        first = project(perm, w_ref[d, :, :256], mask_ref[d], tiles)
        fa[...] = first[:, 0]
        fb[...] = first[:, 1]
        f_to = sends.core if d == 1 else f_core
        sends.to_chips(lambda n: fa.at[n], ra.at[f_slot], *sem[1], f_to)
        project_gate(perm, w_ref[d, :, 512:], gate, d == 1)
        wait_bytes(rs.at[0], sem[0][1])
        copy_s = to_sibling(rs.at[core], on_send.at[d], on_recv.at[d])
        sends.to_chips(lambda n: fb.at[n], rb.at[f_slot], *sem[2], f_to)
        copy_s.wait()
        if d == 0:
            load_n = lambda k: rs[core if k < 8 else 1 - core, k % 8]
            load_a = lambda k: ra[core if k < 8 else 1 - core, k % 8]
            load_b = lambda k: rb[core if k < 8 else 1 - core, k % 8]
        else:
            load_n = lambda k: jnp.stack([rs[n % 2, k, n // 2] for n in range(16)], axis=0)
            load_a = lambda k: ra[k]
            load_b = lambda k: rb[k]
        assemble_right(load_n, right, part)
        wait_bytes(ra, sem[1][1])
        multiply(load_a, 0, left, right, oa)
        sends.to_owners(oa, ba.at[index], *sem[3])
        wait_bytes(rb, sem[2][1])
        multiply(load_b, 1, left, right, ob)
        sends.to_owners(ob, bb.at[index], *sem[4])
        if d == 0:
            loads[2].wait()
        wait_bytes(ba, sem[3][1])
        finish(field, gate, ba, wo_ref[d], tiles, 0)
        wait_bytes(bb, sem[4][1])
        finish(field, gate, bb, wo_ref[d], tiles, 1)
        sends.sent(s_ref, sem[0][0], False)
        sends.sent(fa, sem[1][0], d == 0)
        sends.sent(fb, sem[2][0], d == 0)
        sends.sent(ba, sem[3][0], True)
        sends.sent(bb, sem[4][0], True)
    for i in range(TOK):
        out_ref[i] = field[pl.ds(i * TOK, TOK)].astype(BF)


def per_device(pair, token_mask, chain_ids, chain_bias, in_weights, out_weights):
    hbm = pl.BlockSpec(memory_space=pl.ANY)
    smem = pl.BlockSpec(memory_space=pltpu.SMEM)
    vmem = pl.BlockSpec(memory_space=pltpu.VMEM)
    dma = pltpu.SemaphoreType.DMA
    tokens = pltpu.VMEM((TOK * TOK, CH), F32)
    half = lambda *dims: pltpu.VMEM(dims + (8, 128), BF)
    return pl.pallas_call(
        kernel,
        out_shape=jax.ShapeDtypeStruct((TOK, TOK, CH), BF),
        in_specs=[hbm, smem, smem, vmem, hbm, hbm],
        out_specs=vmem,
        scratch_shapes=[
            pltpu.VMEM((TOK, TOK, CH), BF),
            pltpu.VMEM((2, CH, 5 * CH), BF),
            pltpu.VMEM((2, CH, CH), BF),
            pltpu.VMEM((2, 16, 128), F32),
            pltpu.VMEM((TOK, CH), jnp.int32),
            tokens,
            tokens,
            tokens,
            pltpu.VMEM((PERM, CH), F32),
            pltpu.VMEM((PERM, CH), F32),
            half(CH),
            half(CH),
            half(CH, 2),
            half(16, 8),
            half(16, 8),
            half(2, 8, 8),
            half(2, 8, 8),
            half(2, 8, 16, 2),
            half(16, 8),
            half(16, 8),
            half(2, 16, 8, 2),
            half(CH),
            half(CH),
            half(CH),
            half(CH),
            pltpu.VMEM((192, 768), BF),
            pltpu.VMEM((768, 768), BF),
            pltpu.VMEM((768, 128), F32),
            dma((3,)),
            pltpu.SemaphoreType.REGULAR,
            dma((10,)),
            dma((10,)),
            dma((2,)),
            dma((2,)),
        ],
        compiler_params=pltpu.CompilerParams(
            collective_id=0, has_side_effects=True, vmem_limit_bytes=VMEM_LIMIT
        ),
        cost_estimate=pl.CostEstimate(flops=10**9, bytes_accessed=2 * 10**6, transcendentals=10**6),
        name="pairformer",
    )(pair, token_mask, chain_ids, chain_bias.reshape(1, CH), in_weights, out_weights)


def solution(mesh):
    return jax.shard_map(
        per_device,
        mesh=mesh,
        in_specs=(P("row", "col", None), P(), P(), P(), P(), P()),
        out_specs=P("row", "col", None),
        check_vma=False,
    )
```

```python
import jax
import jax.numpy as jnp
from jax import lax
from jax.experimental import pallas as pl
from jax.experimental.pallas import tpu as pltpu
from jax.sharding import PartitionSpec as P


MESH = pl.DeviceIdType.MESH
TOK = 40
ROWS = 16
PLANE = 8
CHIPS = ROWS * PLANE
CH = 128
DEPTH = 14
PERM = DEPTH * 128
HALVES = ((0, 8), (8, 6))
BF = jnp.bfloat16
F32 = jnp.float32
VMEM_LIMIT = 60 * 2**20
STEPS_Y = (2, 1, 3, 0)
STEPS_Z = (4, 0, 3, 5, 1, 7, 2, 6)
GROUPS = ((0, 1, 2), (3, 4, 5), (6, 7), (8, 9, 10), (11, 12, 13), (14, 15))


def sigmoid(x):
    return 0.5 * jnp.tanh(0.5 * x) + 0.5


def norm_lanes(x):
    center = x - jnp.mean(x, axis=-1, keepdims=True)
    spread = jnp.mean(center * center, axis=-1, keepdims=True)
    return center * lax.rsqrt(spread + 1e-05)


def start_field(pair_ref, ids_ref, bias_ref, field_ref, column):
    row, col = lax.axis_index("row"), lax.axis_index("col")
    for j in range(TOK):
        column[j : j + 1, :] = jnp.full((1, CH), ids_ref[col * TOK + j], jnp.int32)
    bias = bias_ref[...]
    cols = column[...]
    for i in range(TOK):
        same = cols == ids_ref[row * TOK + i]
        field_ref[pl.ds(i * TOK, TOK)] = pair_ref[i].astype(F32) + jnp.where(same, bias, 0.0)


def tile_masks(valid_ref, mask):
    row, col = lax.axis_index("row"), lax.axis_index("col")
    lane = lax.broadcasted_iota(jnp.int32, (1, 128), 1)
    third = (lane >= TOK).astype(jnp.int32) + (lane >= 2 * TOK).astype(jnp.int32)
    place_b = jnp.where(lane < 3 * TOK, lane - TOK * third, TOK)
    rows = [valid_ref[row * TOK + n].astype(F32) for n in range(TOK)]
    cols = [valid_ref[col * TOK + n].astype(F32) for n in range(TOK)]
    for d, (a_valid, b_valid) in enumerate(((rows, cols), (cols, rows))):
        along = jnp.zeros((1, 128), F32)
        for b in range(TOK):
            along = jnp.where(place_b == b, b_valid[b], along)
        for g in range(DEPTH):
            low = jnp.where(third == 0, a_valid[g], a_valid[DEPTH + g])
            high = a_valid[2 * DEPTH + g] if 2 * DEPTH + g < TOK else 0.0
            mask[d, g : g + 1, :] = jnp.where(third == 2, high, low) * along


def arrange(field_ref, nat, perm, swap):
    nat[...] = norm_lanes(field_ref[...])
    for g in range(DEPTH):
        for q in range(3):
            a = DEPTH * q + g
            at = pl.ds(g * 128 + TOK * q, TOK)
            if a >= TOK:
                perm[at] = jnp.zeros((TOK, CH), F32)
            elif swap:
                perm[at] = nat[pl.ds(a, TOK, stride=TOK)]
            else:
                perm[at] = nat[pl.ds(a * TOK, TOK)]
        perm[pl.ds(g * 128 + 120, 8)] = jnp.zeros((8, CH), F32)


def project(perm, w, mask, tiles):
    weights_t = jnp.transpose(w.astype(F32)).astype(BF)
    for lo in range(0, DEPTH, 4):
        count = min(4, DEPTH - lo)
        normed = perm[pl.ds(lo * 128, count * 128)].astype(BF)
        both = lax.dot_general(weights_t, normed, (((1,), (1,)), ((), ())), preferred_element_type=F32)
        value = sigmoid(both[:CH]) * both[CH:]
        for n in range(count):
            g = lo + n
            tiles[pl.ds(g, CH, stride=DEPTH)] = value[:, n * 128 : n * 128 + 128] * mask[g : g + 1, :]
    return tiles[pl.ds(0, CH * DEPTH)].astype(BF).reshape(CH, 7, 2, 128)


def project_gate(perm, w, gate_ref, swap):
    for lo in range(0, DEPTH, 4):
        count = min(4, DEPTH - lo)
        normed = perm[pl.ds(lo * 128, count * 128)].astype(BF)
        value = sigmoid(jnp.dot(normed, w, preferred_element_type=F32))
        for n in range(count):
            for q in range(3):
                a = DEPTH * q + lo + n
                if a < TOK:
                    piece = value[n * 128 + q * TOK : n * 128 + q * TOK + TOK]
                    if swap:
                        gate_ref[pl.ds(a, TOK, stride=TOK)] = piece
                    else:
                        gate_ref[pl.ds(a * TOK, TOK)] = piece


def finish(field_ref, gate_ref, r_ref, weights, tiles, half):
    lo, depth = HALVES[half]
    x = r_ref[...].astype(F32).reshape(CH, depth, 128)
    center = x - jnp.mean(x, axis=0, keepdims=True)
    spread = jnp.mean(center * center, axis=0, keepdims=True)
    tiles[pl.ds(0, CH * depth)] = (center * lax.rsqrt(spread + 1e-05)).reshape(CH * depth, 128)
    for g in range(depth):
        normed = tiles[pl.ds(g, CH, stride=depth)].astype(BF)
        out = lax.dot_general(normed, weights, (((0,), (0,)), ((), ())), preferred_element_type=F32)
        for q in range(3):
            a = DEPTH * q + lo + g
            if a < TOK:
                at = pl.ds(a * TOK, TOK)
                field_ref[at] = field_ref[at] + gate_ref[at] * out[q * TOK : q * TOK + TOK]


def lanes_between(lo, hi, rows):
    lane = lax.broadcasted_iota(jnp.int32, (rows, 128), 1)
    return (lane >= lo) & (lane < hi)


def roll(x, amount):
    amount = amount % 128
    return pltpu.roll(x, amount, 1) if amount else x


def spread_lanes(blocks, q, rows):
    total = jnp.zeros((rows, 128), F32)
    for m, block in enumerate(blocks):
        total = jnp.where(lanes_between(TOK * m, TOK * m + TOK, rows), roll(block, TOK * (m - q)), total)
    return total


def assemble_right(load_n, right, part):
    part[...] = jnp.zeros((768, 128), F32)
    for group, blocks in enumerate(GROUPS):
        parts = [load_n(k).astype(F32).reshape(16 * DEPTH, 128) for k in blocks]
        for q in range(3):
            value = spread_lanes(parts, q, 16 * DEPTH)
            for n in range(16):
                depth = min(DEPTH, TOK - DEPTH * q)
                at = pl.ds(128 * (n // 3) + TOK * (n % 3) + DEPTH * q, depth)
                part[at] = value[n * DEPTH : n * DEPTH + depth]
        right[:, pl.ds(group * 128, 128)] = part[...].astype(BF)


def multiply(load_m, half, left, right, out_ref):
    size = 8 * HALVES[half][1]
    for group, blocks in enumerate(GROUPS):
        parts = [load_m(k).astype(F32).reshape(size, 128) for k in blocks]
        for q in range(3):
            left[pl.ds(q * size, size), pl.ds(group * 128, 128)] = spread_lanes(parts, q, size).astype(BF)
    rows = left[pl.ds(0, 3 * size)]
    total = lax.dot_general(rows, right[...], (((1,), (1,)), ((), ())), preferred_element_type=F32)
    for n in range(16):
        n3, m = n // 3, n % 3
        value = jnp.zeros((size, 128), F32)
        for q in range(3):
            value = jnp.where(
                lanes_between(TOK * q, TOK * q + TOK, size),
                roll(total[q * size : q * size + size, n3 * 128 : n3 * 128 + 128], TOK * (q - m)),
                value,
            )
        out_ref[n] = value.astype(BF).reshape(8, size // 16, 2, 128)


def place():
    row, col = lax.axis_index("row"), lax.axis_index("col")
    return row, col // 2, col % 2


def greet(line):
    row, chip, core = place()
    barrier = pltpu.get_barrier_semaphore()
    chips = [(chip + step) % PLANE for step in range(1, PLANE)]
    for step in range(1, ROWS):
        for other in (core, 1 - core):
            pl.semaphore_signal(
                barrier, inc=1, device_id=((row + step) % ROWS, chip * 2 + other), device_id_type=MESH
            )
    for to_chip in chips:
        pl.semaphore_signal(barrier, inc=1, device_id=(row, to_chip * 2 + core), device_id_type=MESH)
    pl.semaphore_signal(barrier, inc=1, device_id=(row, chip * 2 + 1 - core), device_id_type=MESH)

    def arrived():
        pl.semaphore_wait(barrier, 2 * (ROWS - 1) + PLANE)
        for to_chip in chips:
            pl.semaphore_signal(line, inc=1, device_id=(row, to_chip * 2 + core), device_id_type=MESH)

    return arrived


def remote(src, dst, send_sem, recv_sem, to_row, to_col):
    return pltpu.make_async_remote_copy(
        src_ref=src,
        dst_ref=dst,
        send_sem=send_sem,
        recv_sem=recv_sem,
        device_id=(to_row, to_col),
        device_id_type=MESH,
    )


class Sends:
    def __init__(self):
        self.row, self.chip, self.core = place()
        self.x, y, z_hi, z_lo = self.row // 4, self.chip // 2, self.row % 4, self.chip % 2
        z = [z_hi * 2 + z_lo] + [(z_hi * 2 + z_lo + step) % 8 for step in range(1, 8)]
        self.y = [y * 2] + [(y + step) % 4 * 2 for step in range(1, 4)]
        self.z = [(value // 2, value % 2) for value in z]
        self.z_own = [
            (self.core + 2 * ((z_hi // 2 + s) % 2), (z_lo + t) % 2) for s, t in ((1, 0), (0, 0), (1, 1), (0, 1))
        ]

    def every(self, visit):
        def along(step, carry):
            for dy in STEPS_Y:
                visit((self.x + step) % 4, dy, False)
            return carry

        lax.fori_loop(1, 4, along, 0)
        for dy in STEPS_Y:
            visit(self.x, dy, dy == 0)

    def to_chips(self, src, dst, send_sem, recv_sem, to_core):
        def visit(x, dy, line):
            for dz in STEPS_Z:
                to_row, to_chip = x * 4 + self.z[dz][0], self.y[dy] + self.z[dz][1]
                if not (line and dz == 0):
                    remote(
                        src(to_row * PLANE + to_chip), dst, send_sem, recv_sem, to_row, to_chip * 2 + to_core
                    ).start()

        self.every(visit)
        self.own(src(self.row * PLANE + self.chip), dst, send_sem, recv_sem, self.row, self.chip * 2 + to_core, to_core)

    def own(self, src, dst, send_sem, recv_sem, to_row, to_col, to_core):
        if to_core is self.core:
            pltpu.make_async_copy(src, dst, recv_sem).start()
            return

        @pl.when(to_core == self.core)
        def _():
            pltpu.make_async_copy(src, dst, recv_sem).start()

        @pl.when(to_core != self.core)
        def _():
            remote(src, dst, send_sem, recv_sem, to_row, to_col).start()

    def to_owners(self, o_ref, dst, send_sem, recv_sem):
        parity = self.row % 2

        def visit(x, dy, line):
            for n, (z_hi, z_lo) in enumerate(self.z_own):
                to_row, to_chip = x * 4 + z_hi, self.y[dy] + z_lo
                for other in (0, 1):
                    to_col = to_chip * 2 + (1 - self.core if other else self.core)
                    src = o_ref.at[to_col, to_row // 2]
                    copy = remote(src, dst, send_sem, recv_sem, to_row, to_col)
                    if line and n == 1 and not other:

                        @pl.when(parity == self.core)
                        def _():
                            pltpu.make_async_copy(src, dst, recv_sem).start()

                        @pl.when(parity != self.core)
                        def _():
                            copy.start()

                    else:
                        copy.start()

        self.every(visit)

    def sent(self, ref, send_sem, across):
        wait_bytes(ref.at[pl.ds(0, CHIPS - 1)], send_sem)
        if across:

            @pl.when(self.row % 2 != self.core)
            def _():
                wait_bytes(ref.at[0], send_sem)


def wait_bytes(ref, sem):
    pltpu.make_async_copy(ref, ref, sem).wait()


def to_sibling(ref, send_sem, recv_sem):
    row, chip, core = place()
    copy = remote(ref, ref, send_sem, recv_sem, row, chip * 2 + 1 - core)
    copy.start()
    return copy


def kernel(
    pair_hbm, valid_ref, ids_ref, bias_ref, w_hbm, wo_hbm, out_ref,
    pair_ref, w_ref, wo_ref, mask_ref, column, field, gate, nat, perm, tiles, fa, fb, s_ref, oa, ob,
    ra_out, rb_out, rs_out, ra_in, rb_in, rs_in, ba_out, bb_out, ba_in, bb_in, left, right, part,
    load_sem, line, send_sem, recv_sem, on_send, on_recv,
):
    row, chip, core = place()
    index = row * PLANE + chip
    loads = [
        pltpu.make_async_copy(src, dst, load_sem.at[n])
        for n, (src, dst) in enumerate(((pair_hbm, pair_ref), (w_hbm, w_ref), (wo_hbm, wo_ref)))
    ]
    for load in loads:
        load.start()
    arrived = greet(line)
    sends = Sends()
    tile_masks(valid_ref, mask_ref)
    loads[0].wait()
    start_field(pair_ref, ids_ref, bias_ref, field, column)

    for d in range(2):
        ra, rb, rs, ba, bb = ((ra_out, rb_out, rs_out, ba_out, bb_out), (ra_in, rb_in, rs_in, ba_in, bb_in))[d]
        sem = [(send_sem.at[5 * d + n], recv_sem.at[5 * d + n]) for n in range(5)]
        if d == 0:
            f_core, f_slot, s_slot = row % 2, (core, chip, row // 2), (core, chip, row)
        else:
            f_core, f_slot, s_slot = core, (row, chip), (core, row, chip)
        arrange(field, nat, perm, d == 1)
        if d == 0:
            arrived()
            loads[1].wait()
        s_ref[...] = project(perm, w_ref[d, :, 256:512], mask_ref[d], tiles)
        if d == 0:
            pl.semaphore_wait(line, PLANE - 1)
        sends.to_chips(lambda n: s_ref.at[n], rs.at[s_slot], *sem[0], sends.core)
        first = project(perm, w_ref[d, :, :256], mask_ref[d], tiles)
        fa[...] = first[:, :4]
        fb[...] = first[:, 4:]
        f_to = sends.core if d == 1 else f_core
        sends.to_chips(lambda n: fa.at[n], ra.at[f_slot], *sem[1], f_to)
        project_gate(perm, w_ref[d, :, 512:], gate, d == 1)
        wait_bytes(rs.at[0], sem[0][1])
        copy_s = to_sibling(rs.at[core], on_send.at[d], on_recv.at[d])
        sends.to_chips(lambda n: fb.at[n], rb.at[f_slot], *sem[2], f_to)
        copy_s.wait()
        if d == 0:
            load_n = lambda k: rs[core if k < 8 else 1 - core, k % 8]
            load_a = lambda k: ra[core if k < 8 else 1 - core, k % 8]
            load_b = lambda k: rb[core if k < 8 else 1 - core, k % 8]
        else:
            load_n = lambda k: jnp.stack([rs[n % 2, k, n // 2] for n in range(16)], axis=0)
            load_a = lambda k: ra[k]
            load_b = lambda k: rb[k]
        assemble_right(load_n, right, part)
        wait_bytes(ra, sem[1][1])
        multiply(load_a, 0, left, right, oa)
        sends.to_owners(oa, ba.at[index], *sem[3])
        wait_bytes(rb, sem[2][1])
        multiply(load_b, 1, left, right, ob)
        sends.to_owners(ob, bb.at[index], *sem[4])
        if d == 0:
            loads[2].wait()
        wait_bytes(ba, sem[3][1])
        finish(field, gate, ba, wo_ref[d], tiles, 0)
        wait_bytes(bb, sem[4][1])
        finish(field, gate, bb, wo_ref[d], tiles, 1)
        sends.sent(s_ref, sem[0][0], False)
        sends.sent(fa, sem[1][0], d == 0)
        sends.sent(fb, sem[2][0], d == 0)
        sends.sent(ba, sem[3][0], True)
        sends.sent(bb, sem[4][0], True)
    for i in range(TOK):
        out_ref[i] = field[pl.ds(i * TOK, TOK)].astype(BF)


def per_device(pair, token_mask, chain_ids, chain_bias, in_weights, out_weights):
    hbm = pl.BlockSpec(memory_space=pl.ANY)
    smem = pl.BlockSpec(memory_space=pltpu.SMEM)
    vmem = pl.BlockSpec(memory_space=pltpu.VMEM)
    dma = pltpu.SemaphoreType.DMA
    tokens = pltpu.VMEM((TOK * TOK, CH), F32)
    pairs = lambda count, *dims: pltpu.VMEM(dims + (count, 2, 128), BF)
    low, high, whole = (lambda *dims, count=count: pairs(count, *dims) for count in (4, 3, 7))
    return pl.pallas_call(
        kernel,
        out_shape=jax.ShapeDtypeStruct((TOK, TOK, CH), BF),
        in_specs=[hbm, smem, smem, vmem, hbm, hbm],
        out_specs=vmem,
        scratch_shapes=[
            pltpu.VMEM((TOK, TOK, CH), BF),
            pltpu.VMEM((2, CH, 5 * CH), BF),
            pltpu.VMEM((2, CH, CH), BF),
            pltpu.VMEM((2, 16, 128), F32),
            pltpu.VMEM((TOK, CH), jnp.int32),
            tokens,
            tokens,
            tokens,
            pltpu.VMEM((PERM, CH), F32),
            pltpu.VMEM((PERM, CH), F32),
            low(CH),
            high(CH),
            whole(CH),
            low(16, 8),
            high(16, 8),
            low(2, 8, 8),
            high(2, 8, 8),
            whole(2, 8, 16),
            low(16, 8),
            high(16, 8),
            whole(2, 16, 8),
            low(CH),
            high(CH),
            low(CH),
            high(CH),
            pltpu.VMEM((192, 768), BF),
            pltpu.VMEM((768, 768), BF),
            pltpu.VMEM((768, 128), F32),
            dma((3,)),
            pltpu.SemaphoreType.REGULAR,
            dma((10,)),
            dma((10,)),
            dma((2,)),
            dma((2,)),
        ],
        compiler_params=pltpu.CompilerParams(
            collective_id=0, has_side_effects=True, vmem_limit_bytes=VMEM_LIMIT
        ),
        cost_estimate=pl.CostEstimate(flops=10**9, bytes_accessed=2 * 10**6, transcendentals=10**6),
        name="pairformer",
    )(pair, token_mask, chain_ids, chain_bias.reshape(1, CH), in_weights, out_weights)


def solution(mesh):
    return jax.shard_map(
        per_device,
        mesh=mesh,
        in_specs=(P("row", "col", None), P(), P(), P(), P(), P()),
        out_specs=P("row", "col", None),
        check_vma=False,
    )
```

```python
import jax
import jax.numpy as jnp
from jax import lax
from jax.experimental import pallas as pl
from jax.experimental.pallas import tpu as pltpu
from jax.sharding import PartitionSpec as P


MESH = pl.DeviceIdType.MESH
TOK = 40
ROWS = 16
PLANE = 8
CHIPS = ROWS * PLANE
CH = 128
DEPTH = 14
PERM = DEPTH * 128
HALVES = ((0, 8), (8, 6))
BF = jnp.bfloat16
F32 = jnp.float32
VMEM_LIMIT = 60 * 2**20
STEPS_Y = (2, 1, 3, 0)
STEPS_Z = (4, 0, 3, 5, 1, 7, 2, 6)
GROUPS = ((0, 1, 2), (3, 4, 5), (6, 7), (8, 9, 10), (11, 12, 13), (14, 15))


def sigmoid(x):
    return 0.5 * jnp.tanh(0.5 * x) + 0.5


def norm_lanes(x):
    center = x - jnp.mean(x, axis=-1, keepdims=True)
    spread = jnp.mean(center * center, axis=-1, keepdims=True)
    return center * lax.rsqrt(spread + 1e-05)


def start_field(pair_ref, ids_ref, bias_ref, field_ref, column):
    row, col = lax.axis_index("row"), lax.axis_index("col")
    for j in range(TOK):
        column[j : j + 1, :] = jnp.full((1, CH), ids_ref[col * TOK + j], jnp.int32)
    bias = bias_ref[...]
    cols = column[...]
    for i in range(TOK):
        same = cols == ids_ref[row * TOK + i]
        field_ref[pl.ds(i * TOK, TOK)] = pair_ref[i].astype(F32) + jnp.where(same, bias, 0.0)


def tile_masks(valid_ref, mask):
    row, col = lax.axis_index("row"), lax.axis_index("col")
    lane = lax.broadcasted_iota(jnp.int32, (1, 128), 1)
    third = (lane >= TOK).astype(jnp.int32) + (lane >= 2 * TOK).astype(jnp.int32)
    place_b = jnp.where(lane < 3 * TOK, lane - TOK * third, TOK)
    rows = [valid_ref[row * TOK + n].astype(F32) for n in range(TOK)]
    cols = [valid_ref[col * TOK + n].astype(F32) for n in range(TOK)]
    for d, (a_valid, b_valid) in enumerate(((rows, cols), (cols, rows))):
        along = jnp.zeros((1, 128), F32)
        for b in range(TOK):
            along = jnp.where(place_b == b, b_valid[b], along)
        for g in range(DEPTH):
            low = jnp.where(third == 0, a_valid[g], a_valid[DEPTH + g])
            high = a_valid[2 * DEPTH + g] if 2 * DEPTH + g < TOK else 0.0
            mask[d, g : g + 1, :] = jnp.where(third == 2, high, low) * along


def arrange(field_ref, nat, perm, swap):
    nat[...] = norm_lanes(field_ref[...])
    for g in range(DEPTH):
        for q in range(3):
            a = DEPTH * q + g
            at = pl.ds(g * 128 + TOK * q, TOK)
            if a >= TOK:
                perm[at] = jnp.zeros((TOK, CH), F32)
            elif swap:
                perm[at] = nat[pl.ds(a, TOK, stride=TOK)]
            else:
                perm[at] = nat[pl.ds(a * TOK, TOK)]
        perm[pl.ds(g * 128 + 120, 8)] = jnp.zeros((8, CH), F32)


def project(perm, w, mask, tiles):
    weights_t = jnp.transpose(w.astype(F32)).astype(BF)
    for lo in range(0, DEPTH, 4):
        count = min(4, DEPTH - lo)
        normed = perm[pl.ds(lo * 128, count * 128)].astype(BF)
        both = lax.dot_general(weights_t, normed, (((1,), (1,)), ((), ())), preferred_element_type=F32)
        value = sigmoid(both[:CH]) * both[CH:]
        for n in range(count):
            g = lo + n
            tiles[pl.ds(g, CH, stride=DEPTH)] = value[:, n * 128 : n * 128 + 128] * mask[g : g + 1, :]
    return tiles[pl.ds(0, CH * DEPTH)].astype(BF).reshape(CH, 7, 2, 128)


def project_gate(perm, w, gate_ref, swap):
    for lo in range(0, DEPTH, 4):
        count = min(4, DEPTH - lo)
        normed = perm[pl.ds(lo * 128, count * 128)].astype(BF)
        value = sigmoid(jnp.dot(normed, w, preferred_element_type=F32))
        for n in range(count):
            for q in range(3):
                a = DEPTH * q + lo + n
                if a < TOK:
                    piece = value[n * 128 + q * TOK : n * 128 + q * TOK + TOK]
                    if swap:
                        gate_ref[pl.ds(a, TOK, stride=TOK)] = piece
                    else:
                        gate_ref[pl.ds(a * TOK, TOK)] = piece


def finish(field_ref, gate_ref, r_ref, weights, tiles, half):
    lo, depth = HALVES[half]
    x = r_ref[...].astype(F32).reshape(CH, depth, 128)
    center = x - jnp.mean(x, axis=0, keepdims=True)
    spread = jnp.mean(center * center, axis=0, keepdims=True)
    tiles[pl.ds(0, CH * depth)] = (center * lax.rsqrt(spread + 1e-05)).reshape(CH * depth, 128)
    for g in range(depth):
        normed = tiles[pl.ds(g, CH, stride=depth)].astype(BF)
        out = lax.dot_general(normed, weights, (((0,), (0,)), ((), ())), preferred_element_type=F32)
        for q in range(3):
            a = DEPTH * q + lo + g
            if a < TOK:
                at = pl.ds(a * TOK, TOK)
                field_ref[at] = field_ref[at] + gate_ref[at] * out[q * TOK : q * TOK + TOK]


def lanes_between(lo, hi, rows):
    lane = lax.broadcasted_iota(jnp.int32, (rows, 128), 1)
    return (lane >= lo) & (lane < hi)


def roll(x, amount):
    amount = amount % 128
    return pltpu.roll(x, amount, 1) if amount else x


def spread_lanes(blocks, q, rows):
    total = jnp.zeros((rows, 128), F32)
    for m, block in enumerate(blocks):
        total = jnp.where(lanes_between(TOK * m, TOK * m + TOK, rows), roll(block, TOK * (m - q)), total)
    return total


def assemble_right(load_n, groups, blocks_n, rows, right, part):
    size = len(blocks_n) * DEPTH
    for group in groups:
        parts = [load_n(k).astype(F32).reshape(size, 128) for k in GROUPS[group]]
        for q in range(3):
            value = spread_lanes(parts, q, size)
            for place_n, n in enumerate(blocks_n):
                depth = min(DEPTH, TOK - DEPTH * q)
                at = pl.ds(128 * (n // 3) + TOK * (n % 3) + DEPTH * q, depth)
                part[at] = value[place_n * DEPTH : place_n * DEPTH + depth]
        right[rows, pl.ds(group * 128, 128)] = part[rows].astype(BF)


def multiply(load_m, half, left, right, out_ref):
    size = 8 * HALVES[half][1]
    for group, blocks in enumerate(GROUPS):
        parts = [load_m(k).astype(F32).reshape(size, 128) for k in blocks]
        for q in range(3):
            left[pl.ds(q * size, size), pl.ds(group * 128, 128)] = spread_lanes(parts, q, size).astype(BF)
    rows = left[pl.ds(0, 3 * size)]
    total = lax.dot_general(rows, right[...], (((1,), (1,)), ((), ())), preferred_element_type=F32)
    for n in range(16):
        n3, m = n // 3, n % 3
        value = jnp.zeros((size, 128), F32)
        for q in range(3):
            value = jnp.where(
                lanes_between(TOK * q, TOK * q + TOK, size),
                roll(total[q * size : q * size + size, n3 * 128 : n3 * 128 + 128], TOK * (q - m)),
                value,
            )
        out_ref[n] = value.astype(BF).reshape(8, size // 16, 2, 128)


def place():
    row, col = lax.axis_index("row"), lax.axis_index("col")
    return row, col // 2, col % 2


def greet(line):
    row, chip, core = place()
    barrier = pltpu.get_barrier_semaphore()
    chips = [(chip + step) % PLANE for step in range(1, PLANE)]
    for step in range(1, ROWS):
        for other in (core, 1 - core):
            pl.semaphore_signal(
                barrier, inc=1, device_id=((row + step) % ROWS, chip * 2 + other), device_id_type=MESH
            )
    for to_chip in chips:
        pl.semaphore_signal(barrier, inc=1, device_id=(row, to_chip * 2 + core), device_id_type=MESH)
    pl.semaphore_signal(barrier, inc=1, device_id=(row, chip * 2 + 1 - core), device_id_type=MESH)

    def arrived():
        pl.semaphore_wait(barrier, 2 * (ROWS - 1) + PLANE)
        for to_chip in chips:
            pl.semaphore_signal(line, inc=1, device_id=(row, to_chip * 2 + core), device_id_type=MESH)

    return arrived


def remote(src, dst, send_sem, recv_sem, to_row, to_col):
    return pltpu.make_async_remote_copy(
        src_ref=src,
        dst_ref=dst,
        send_sem=send_sem,
        recv_sem=recv_sem,
        device_id=(to_row, to_col),
        device_id_type=MESH,
    )


class Sends:
    def __init__(self):
        self.row, self.chip, self.core = place()
        self.x, y, z_hi, z_lo = self.row // 4, self.chip // 2, self.row % 4, self.chip % 2
        z = [z_hi * 2 + z_lo] + [(z_hi * 2 + z_lo + step) % 8 for step in range(1, 8)]
        self.y = [y * 2] + [(y + step) % 4 * 2 for step in range(1, 4)]
        self.z = [(value // 2, value % 2) for value in z]
        self.z_own = [
            (self.core + 2 * ((z_hi // 2 + s) % 2), (z_lo + t) % 2) for s, t in ((1, 0), (0, 0), (1, 1), (0, 1))
        ]

    def every(self, visit):
        def along(step, carry):
            for dy in STEPS_Y:
                visit((self.x + step) % 4, dy, False)
            return carry

        lax.fori_loop(1, 4, along, 0)
        for dy in STEPS_Y:
            visit(self.x, dy, dy == 0)

    def to_chips(self, src, dst, send_sem, recv_sem, to_core):
        def visit(x, dy, line):
            for dz in STEPS_Z:
                to_row, to_chip = x * 4 + self.z[dz][0], self.y[dy] + self.z[dz][1]
                if not (line and dz == 0):
                    remote(
                        src(to_row * PLANE + to_chip), dst, send_sem, recv_sem, to_row, to_chip * 2 + to_core
                    ).start()

        self.every(visit)
        self.own(src(self.row * PLANE + self.chip), dst, send_sem, recv_sem, self.row, self.chip * 2 + to_core, to_core)

    def own(self, src, dst, send_sem, recv_sem, to_row, to_col, to_core):
        if to_core is self.core:
            pltpu.make_async_copy(src, dst, recv_sem).start()
            return

        @pl.when(to_core == self.core)
        def _():
            pltpu.make_async_copy(src, dst, recv_sem).start()

        @pl.when(to_core != self.core)
        def _():
            remote(src, dst, send_sem, recv_sem, to_row, to_col).start()

    def to_owners(self, o_ref, slot, dst, send_sem, recv_sem):
        parity = self.row % 2

        def visit(x, dy, line):
            for n, (z_hi, z_lo) in enumerate(self.z_own):
                to_row, to_chip = x * 4 + z_hi, self.y[dy] + z_lo
                for other in (0, 1):
                    to_col = to_chip * 2 + (1 - self.core if other else self.core)
                    src = o_ref.at[slot(to_chip, other, to_col), to_row // 2]
                    copy = remote(src, dst, send_sem, recv_sem, to_row, to_col)
                    if line and n == 1 and not other:

                        @pl.when(parity == self.core)
                        def _():
                            pltpu.make_async_copy(src, dst, recv_sem).start()

                        @pl.when(parity != self.core)
                        def _():
                            copy.start()

                    else:
                        copy.start()

        self.every(visit)

    def sent(self, ref, send_sem, across):
        wait_bytes(ref.at[pl.ds(0, CHIPS - 1)], send_sem)
        if across:

            @pl.when(self.row % 2 != self.core)
            def _():
                wait_bytes(ref.at[0], send_sem)


def wait_bytes(ref, sem):
    pltpu.make_async_copy(ref, ref, sem).wait()


def to_sibling(ref, send_sem, recv_sem):
    row, chip, core = place()
    copy = remote(ref, ref, send_sem, recv_sem, row, chip * 2 + 1 - core)
    copy.start()
    return copy


def kernel(
    pair_hbm, valid_ref, ids_ref, bias_ref, w_hbm, wo_hbm, out_ref,
    pair_ref, w_ref, wo_ref, mask_ref, column, field, gate, nat, perm, tiles, fa, fb, s_ref, oa, ob,
    ra_out, rb_out, rs_out, ra_in, rb_in, rs_in, ba_out, bb_out, ba_in, bb_in, left, right, part,
    load_sem, line, send_sem, recv_sem, on_send, on_recv,
):
    row, chip, core = place()
    index = row * PLANE + chip
    loads = [
        pltpu.make_async_copy(src, dst, load_sem.at[n])
        for n, (src, dst) in enumerate(((pair_hbm, pair_ref), (w_hbm, w_ref), (wo_hbm, wo_ref)))
    ]
    for load in loads:
        load.start()
    arrived = greet(line)
    part[...] = jnp.zeros((768, 128), F32)
    sends = Sends()
    tile_masks(valid_ref, mask_ref)
    loads[0].wait()
    start_field(pair_ref, ids_ref, bias_ref, field, column)

    for d in range(2):
        ra, rb, rs, ba, bb = ((ra_out, rb_out, rs_out, ba_out, bb_out), (ra_in, rb_in, rs_in, ba_in, bb_in))[d]
        sem = [(send_sem.at[5 * d + n], recv_sem.at[5 * d + n]) for n in range(5)]
        if d == 0:
            f_core, f_slot, s_slot = row % 2, (core, chip, row // 2), (core, chip, row)
        else:
            f_core, f_slot, s_slot = core, (row, chip), (core, row, chip)
        arrange(field, nat, perm, d == 1)
        if d == 0:
            arrived()
            loads[1].wait()
        s_ref[...] = project(perm, w_ref[d, :, 256:512], mask_ref[d], tiles)
        if d == 0:
            pl.semaphore_wait(line, PLANE - 1)
        sends.to_chips(lambda n: s_ref.at[n], rs.at[s_slot], *sem[0], sends.core)
        first = project(perm, w_ref[d, :, :256], mask_ref[d], tiles)
        fa[...] = first[:, :4]
        fb[...] = first[:, 4:]
        f_to = sends.core if d == 1 else f_core
        sends.to_chips(lambda n: fa.at[n], ra.at[f_slot], *sem[1], f_to)
        project_gate(perm, w_ref[d, :, 512:], gate, d == 1)
        wait_bytes(rs.at[0], sem[0][1])
        copy_s = to_sibling(rs.at[core], on_send.at[d], on_recv.at[d])
        if d == 0:
            plane = lambda k: core if k < 8 else 1 - core
            load_n = (lambda k: rs[plane(k), k % 8],) * 2
            load_a, load_b = (lambda k: ra[plane(k), k % 8]), (lambda k: rb[plane(k), k % 8])
            shares = ((range(3), range(16), pl.ds(0, 768)), (range(3, 6), range(16), pl.ds(0, 768)))
            slot = lambda to_chip, other, to_col: to_col
        else:
            load_n = (lambda k: rs[core, k], lambda k: rs[1 - core, k])
            load_a, load_b = (lambda k: ra[k]), (lambda k: rb[k])
            shares = ((range(6), range(8), pl.ds(0, 336)), (range(6), range(8, 16), pl.ds(336, 432)))
            slot = lambda to_chip, other, to_col: other * 8 + to_chip
        assemble_right(load_n[0], *shares[0], right, part)
        sends.to_chips(lambda n: fb.at[n], rb.at[f_slot], *sem[2], f_to)
        copy_s.wait()
        assemble_right(load_n[1], *shares[1], right, part)
        wait_bytes(ra, sem[1][1])
        multiply(load_a, 0, left, right, oa)
        sends.to_owners(oa, slot, ba.at[index], *sem[3])
        wait_bytes(rb, sem[2][1])
        multiply(load_b, 1, left, right, ob)
        sends.to_owners(ob, slot, bb.at[index], *sem[4])
        if d == 0:
            loads[2].wait()
        wait_bytes(ba, sem[3][1])
        finish(field, gate, ba, wo_ref[d], tiles, 0)
        wait_bytes(bb, sem[4][1])
        finish(field, gate, bb, wo_ref[d], tiles, 1)
        sends.sent(s_ref, sem[0][0], False)
        sends.sent(fa, sem[1][0], d == 0)
        sends.sent(fb, sem[2][0], d == 0)
        sends.sent(ba, sem[3][0], True)
        sends.sent(bb, sem[4][0], True)
    for i in range(TOK):
        out_ref[i] = field[pl.ds(i * TOK, TOK)].astype(BF)


def per_device(pair, token_mask, chain_ids, chain_bias, in_weights, out_weights):
    hbm = pl.BlockSpec(memory_space=pl.ANY)
    smem = pl.BlockSpec(memory_space=pltpu.SMEM)
    vmem = pl.BlockSpec(memory_space=pltpu.VMEM)
    dma = pltpu.SemaphoreType.DMA
    tokens = pltpu.VMEM((TOK * TOK, CH), F32)
    pairs = lambda count, *dims: pltpu.VMEM(dims + (count, 2, 128), BF)
    low, high, whole = (lambda *dims, count=count: pairs(count, *dims) for count in (4, 3, 7))
    return pl.pallas_call(
        kernel,
        out_shape=jax.ShapeDtypeStruct((TOK, TOK, CH), BF),
        in_specs=[hbm, smem, smem, vmem, hbm, hbm],
        out_specs=vmem,
        scratch_shapes=[
            pltpu.VMEM((TOK, TOK, CH), BF),
            pltpu.VMEM((2, CH, 5 * CH), BF),
            pltpu.VMEM((2, CH, CH), BF),
            pltpu.VMEM((2, 16, 128), F32),
            pltpu.VMEM((TOK, CH), jnp.int32),
            tokens,
            tokens,
            tokens,
            pltpu.VMEM((PERM, CH), F32),
            pltpu.VMEM((PERM, CH), F32),
            low(CH),
            high(CH),
            whole(CH),
            low(16, 8),
            high(16, 8),
            low(2, 8, 8),
            high(2, 8, 8),
            whole(2, 8, 16),
            low(16, 8),
            high(16, 8),
            whole(2, 16, 8),
            low(CH),
            high(CH),
            low(CH),
            high(CH),
            pltpu.VMEM((192, 768), BF),
            pltpu.VMEM((768, 768), BF),
            pltpu.VMEM((768, 128), F32),
            dma((3,)),
            pltpu.SemaphoreType.REGULAR,
            dma((10,)),
            dma((10,)),
            dma((2,)),
            dma((2,)),
        ],
        compiler_params=pltpu.CompilerParams(
            collective_id=0, has_side_effects=True, vmem_limit_bytes=VMEM_LIMIT
        ),
        cost_estimate=pl.CostEstimate(flops=10**9, bytes_accessed=2 * 10**6, transcendentals=10**6),
        name="pairformer",
    )(pair, token_mask, chain_ids, chain_bias.reshape(1, CH), in_weights, out_weights)


def solution(mesh):
    return jax.shard_map(
        per_device,
        mesh=mesh,
        in_specs=(P("row", "col", None), P(), P(), P(), P(), P()),
        out_specs=P("row", "col", None),
        check_vma=False,
    )
```
